32 devices in a mesh: pair: 8 (over z, x), fac: 4 (over y, core).
Axes of the slice: x: 2, y: 2, z: 4, core: 2. Of those that a mesh axis runs over, the one named last changes fastest.
Arguments:
- amplitudes: bfloat16 [32, 1024, 1024], P(('pair', 'fac')), may hold values from -6 to 6
- mirror_slot: int32 [32], P(('pair', 'fac')), may hold values from 0 to 0, as said below
- d_values: bfloat16 [4, 16, 64, 64], P('fac'), may hold values from -0.375 to 0.375
- d_cols: int32 [4, 16], P('fac'), may hold values from 0 to 15
- b_values: bfloat16 [4, 16, 64, 64], P('fac'), may hold values from -0.375 to 0.375
- b_cols: int32 [4, 16], P('fac'), may hold values from 0 to 15
Outputs:
- residual: bfloat16 [32, 1024, 1024], P(('pair', 'fac'))
The draws below stay inside these ranges and needn't reach their ends.
Inputs may be any that keep to these rules, and one draw needn't show every extreme that they name: Mirrors are mutual: the pairs on device pair index p and fac index f have their mirrors on pair index (p + 8/2) mod 8 with the same fac index, and m(m(n)) = n; on each device mirror_slot is a permutation of its 1 slots.
All inputs are finite; a program needn't handle non-finite values.
Results may differ from the reference program's by a relative error of at most 0.0059.
Values may be sent and summed in bfloat16 or wider, within the bound.
No kernel may reach another device: no remote copies, remote signals or barrier semaphores. Data moves between devices by JAX's collectives and lax.ppermute only.
A program may use at most 128 MiB of HBM per device.

```python
import jax
import jax.numpy as jnp
from jax import lax

V = 1024
BS = 64
Q = 4
PAIR_DEV = 1
NBLK = 16
PAIRS = 32
N_PAIR = 8
N_FAC = 4


def draw_mirror_slot(key, part):
    half = N_PAIR // 2
    scores = jax.random.randint(key, (half, N_FAC, PAIR_DEV), 0, 1 << 20) * PAIR_DEV
    scores = scores + jnp.arange(PAIR_DEV, dtype=jnp.int32)
    forward = jnp.argsort(scores, axis=-1).astype(jnp.int32)
    backward = jnp.argsort(forward, axis=-1).astype(jnp.int32)
    joined = jnp.concatenate([forward, backward], axis=0)
    return joined.reshape(PAIRS).astype(jnp.int32)


def plant(array, key, low, largest):
    place = [jax.random.randint(jax.random.fold_in(key, axis), (), 0, length) for axis, length in enumerate(array.shape)]
    longest = array.shape.index(max(array.shape))
    beside = place[:longest] + [(place[longest] + 1) % array.shape[longest]] + place[longest + 1:]
    return array.at[tuple(place)].set(low).at[tuple(beside)].set(largest)


def block_scale(stream_key, dims, shards, smallest, top_value):
    loudness = 1.0
    for dim, parts in shards:
        steps = jax.random.uniform(jax.random.fold_in(jax.random.fold_in(stream_key, 6), dim), (parts,), jnp.float32, smallest / len(shards), top_value / len(shards))
        loudness = loudness * jnp.repeat(jnp.exp(steps), dims[dim] // parts).reshape((-1,) + (1,) * (len(dims) - 1 - dim))
    return loudness


def scatter_about(stream_key, shape, width, limit, split=(), kind=jnp.bfloat16):
    array = width * jax.random.normal(stream_key, shape, jnp.float32)
    if split:
        array = array * block_scale(stream_key, shape, split, -0.22, 0.18)
    return jnp.clip(array, -limit, limit).astype(kind)


def setup_inputs(seed: int = 0) -> dict:
    splits = jax.random.split(jax.random.key(seed), 7)
    amplitudes = scatter_about(splits[0], (PAIRS, V, V), 1.0, 6.0, ((0, 32),))
    mirror_slot = draw_mirror_slot(jax.random.fold_in(splits[6], 71), 0)
    d_values = scatter_about(splits[2], (Q, NBLK, BS, BS), (4 * BS) ** -0.5, 0.375, ((0, 4),))
    d_cols = plant(jax.random.randint(splits[3], (Q, NBLK), 0, NBLK), jax.random.fold_in(splits[3], 1), 0, NBLK - 1).astype(jnp.int32)
    b_values = scatter_about(splits[4], (Q, NBLK, BS, BS), (4 * BS) ** -0.5, 0.375, ((0, 4),))
    b_cols = plant(jax.random.randint(splits[5], (Q, NBLK), 0, NBLK), jax.random.fold_in(splits[5], 1), 0, NBLK - 1).astype(jnp.int32)
    return {"amplitudes": amplitudes, "mirror_slot": mirror_slot, "d_values": d_values, "d_cols": d_cols, "b_values": b_values, "b_cols": b_cols}


def dress_one(amps, d_values, d_cols, b_values, b_cols):
    total = jnp.zeros((V, V), jnp.float32)
    for factor in range(Q):
        blocks = amps.reshape(NBLK, BS, V)
        picked = jnp.take(blocks, d_cols[factor], axis=0)
        left = jnp.einsum('rab,rbv->rav', d_values[factor].astype(jnp.float32), picked.astype(jnp.float32))
        left = left.reshape(V, V).astype(jnp.bfloat16)
        columns = left.reshape(V, NBLK, BS)
        chosen = jnp.take(columns, b_cols[factor], axis=1)
        right = jnp.einsum('arb,rcb->arc', chosen.astype(jnp.float32), b_values[factor].astype(jnp.float32))
        total = total + right.reshape(V, V)
    return total.astype(jnp.bfloat16)


def reference(amplitudes, mirror_slot, d_values, d_cols, b_values, b_cols):
    dressed = lax.map(lambda amps: dress_one(amps, d_values, d_cols, b_values, b_cols), amplitudes)
    index = jnp.arange(PAIRS, dtype=jnp.int32)
    device = index // PAIR_DEV
    pair_pos = device // N_FAC
    fac_pos = device % N_FAC
    partner = ((pair_pos + N_PAIR // 2) % N_PAIR * N_FAC + fac_pos) * PAIR_DEV + mirror_slot
    partner = partner.astype(jnp.int32)

    def finish(which):
        own = lax.dynamic_index_in_dim(dressed, which, 0, keepdims=False)
        other = lax.dynamic_index_in_dim(dressed, partner[which], 0, keepdims=False)
        return (own.astype(jnp.float32) + other.astype(jnp.float32).T).astype(jnp.bfloat16)

    return lax.map(finish, index)
```

```python
import functools

import jax
import jax.numpy as jnp
from jax import lax
from jax.experimental import pallas as pl
from jax.experimental.pallas import tpu as pltpu
from jax.sharding import PartitionSpec as P

LANES = 128
BF16, F32 = jnp.bfloat16, jnp.float32
WHOLE = pl.BlockSpec(memory_space=pltpu.VMEM)
SCALARS = pl.BlockSpec(memory_space=pltpu.SMEM)
ANYWHERE = pl.BlockSpec(memory_space=pl.ANY)
VMEM_BYTES = 28 << 20


def params():
    return pltpu.CompilerParams(vmem_limit_bytes=VMEM_BYTES)


def turn_kernel(marks, source, *turned):
    for lo in range(marks[0], marks[-1], LANES):
        strip = source[0, :, lo - marks[0] : lo - marks[0] + LANES].T
        for first, last, piece in zip(marks, marks[1:], turned):
            a, b = max(lo, first), min(lo + LANES, last)
            if a < b:
                piece[0, a - first : b - first, :] = strip[a - lo : b - lo, :]


def turn(amplitudes, marks):
    size = amplitudes.shape[1]
    return pl.pallas_call(
        functools.partial(turn_kernel, marks),
        in_specs=[WHOLE],
        out_specs=[WHOLE] * (len(marks) - 1),
        out_shape=[jax.ShapeDtypeStruct((1, b - a, size), BF16) for a, b in zip(marks, marks[1:])],
        compiler_params=params(),
        name="turn",
    )(amplitudes[:, :, marks[0] : marks[-1]])


def spread_right(values, columns, side, spread):
    factors, blocks, width = values.shape[0], values.shape[1], values.shape[2]
    spread[...] = jnp.zeros(spread.shape, BF16)

    def one(group, carry):
        for q in range(factors):
            for i in range(2):
                s = 2 * group + i
                row = i * LANES + (columns[q, side, s] % 2) * width
                block = values[q, s].T
                spread[q, group, pl.ds(pl.multiple_of(row, width), width), i * width : (i + 1) * width] = block
        return carry

    lax.fori_loop(0, blocks // 2, one, 0)


def join_left(values, joined):
    factors, blocks, width = values.shape[0], values.shape[1], values.shape[2]

    def one(r, carry):
        for q in range(factors):
            joined[r, :, q * width : (q + 1) * width] = values[q, r]
        return carry

    lax.fori_loop(0, blocks, one, 0)


def apply_right(source, columns, side, spread, middle, first, rows, step):
    factors, groups = spread.shape[0], spread.shape[1]

    def one(q, carry):
        for g in range(groups):
            a = pl.multiple_of(columns[q, side, 2 * g] // 2 * LANES, LANES)
            b = pl.multiple_of(columns[q, side, 2 * g + 1] // 2 * LANES, LANES)
            weights = spread[q, g]
            for m in range(0, rows, step):
                picked = jnp.concatenate([source(m, step, a), source(m, step, b)], axis=1)
                product = jnp.dot(picked, weights, preferred_element_type=F32)
                middle[q, first + m : first + m + step, g * LANES : (g + 1) * LANES] = product.astype(BF16)
        return carry

    lax.fori_loop(0, factors, one, 0)


def apply_left(r, joined, columns, side, middle):
    factors = middle.shape[0]
    width = joined.shape[1]
    picked = [
        middle[q, pl.ds(pl.multiple_of(columns[q, side, r] * width, width), width), :] for q in range(factors)
    ]
    return jnp.dot(joined[r], jnp.concatenate(picked, axis=0), preferred_element_type=F32)


def own_kernel(columns, d_all, b_all, source, dressed, spread_d, joined_b, spread_b, joined_d, middle):
    blocks, width = d_all.shape[1], d_all.shape[2]
    size = source.shape[1]
    spread_right(b_all, columns, 1, spread_b)
    join_left(d_all, joined_d)
    spread_right(d_all, columns, 0, spread_d)
    join_left(b_all, joined_b)
    step = min(256, size)
    apply_right(
        lambda m, rows, lane: source[0, m : m + rows, pl.ds(lane, LANES)], columns, 1, spread_b, middle, 0, size, step
    )

    def one(r, carry):
        block = apply_left(r, joined_d, columns, 0, middle)
        dressed[pl.ds(pl.multiple_of(r * width, width), width), :] = block.astype(BF16)
        return carry

    lax.fori_loop(0, blocks, one, 0)


def own_pair(columns, d_all, b_all, amplitudes):
    factors, blocks, width = d_all.shape[:3]
    size = amplitudes.shape[1]
    spread = (factors, blocks // 2, 2 * LANES, LANES)
    joined = (blocks, width, factors * width)
    return pl.pallas_call(
        own_kernel,
        in_specs=[SCALARS, WHOLE, WHOLE, WHOLE],
        out_specs=[WHOLE] * 3,
        out_shape=[
            pltpu.VMEM((size, size), BF16),
            pltpu.VMEM(spread, BF16),
            pltpu.VMEM(joined, BF16),
        ],
        scratch_shapes=[
            pltpu.VMEM(spread, BF16),
            pltpu.VMEM(joined, BF16),
            pltpu.VMEM((factors, size, size), BF16),
        ],
        compiler_params=params(),
        name="own",
    )(columns, d_all, b_all, amplitudes)


def mirror_kernel(lo, hi, again, columns, slot, piece, spread_d, joined_b, dressed, *rest):
    middle, out, ready, sems = rest[2:] if again else rest
    factors, blocks, width = spread_d.shape[0], joined_b.shape[0], joined_b.shape[1]
    rows = (hi - lo) * width
    step = min(256, rows)
    while rows % step:
        step //= 2
    which = slot[0]
    apply_right(
        lambda m, n, lane: piece[which, m : m + n, pl.ds(lane, LANES)],
        columns,
        0,
        spread_d,
        middle,
        lo * width,
        rows,
        step,
    )

    def last_of(r):
        last = columns[0, 1, r]
        for q in range(1, factors):
            last = jnp.maximum(last, columns[q, 1, r])
        return jnp.logical_and(last >= lo, last < hi)

    def place(r):
        rows = pl.ds(pl.multiple_of(r * width, width), width)
        return pltpu.make_async_copy(ready.at[r], out.at[rows, :], sems.at[r])

    def one(r, carry):
        @pl.when(last_of(r))
        def _():
            rows = pl.ds(pl.multiple_of(r * width, width), width)
            mirrored = apply_left(r, joined_b, columns, 1, middle).astype(BF16)
            ready[r] = (dressed[rows, :].astype(F32) + mirrored.astype(F32)).astype(BF16)
            place(r).start()

        return carry

    def wait(r, carry):
        @pl.when(last_of(r))
        def _():
            place(r).wait()

        return carry

    lax.fori_loop(0, blocks, one, 0)
    lax.fori_loop(0, blocks, wait, 0)


def mirror_piece(lo, hi, columns, slot, piece, spread_d, joined_b, dressed, state):
    factors, blocks, width = spread_d.shape[0], joined_b.shape[0], joined_b.shape[1]
    size = dressed.shape[0]
    again = state is not None
    state = state or ()
    middle = pltpu.VMEM((factors, size, size), BF16)
    return pl.pallas_call(
        functools.partial(mirror_kernel, lo, hi, again),
        in_specs=[SCALARS, SCALARS, WHOLE, WHOLE, WHOLE, WHOLE] + ([WHOLE, ANYWHERE] if again else []),
        out_specs=[WHOLE, ANYWHERE],
        out_shape=[middle, jax.ShapeDtypeStruct((size, size), BF16)],
        scratch_shapes=[pltpu.VMEM((blocks, width, size), BF16), pltpu.SemaphoreType.DMA((blocks,))],
        input_output_aliases={6: 0, 7: 1} if again else {},
        compiler_params=params(),
        name="mirror",
    )(columns, slot, piece, spread_d, joined_b, dressed, *state)


def cuts(blocks):
    marks = [0, 4, 10, 14, 15, 16]
    return [m * blocks // 16 for m in marks]


def shards(amplitudes, mirror_slot, d_values, d_cols, b_values, b_cols):
    pairs = lax.axis_size("pair")
    perm = [(i, (i + pairs // 2) % pairs) for i in range(pairs)]
    count, size = amplitudes.shape[0], amplitudes.shape[1]
    assert count == 1
    blocks, width = d_values.shape[1], d_values.shape[2]

    marks = cuts(blocks)
    lanes = [m * width for m in marks]
    turned = turn(amplitudes, lanes[:2]) + turn(amplitudes, lanes[1:])

    columns = jnp.stack([d_cols, b_cols], axis=1)
    turned, columns, d_values, b_values = lax.optimization_barrier((turned, columns, d_values, b_values))
    pieces = [lax.ppermute(piece, "pair", perm) for piece in turned]
    columns, d_all, b_all = (lax.all_gather(a, "fac", axis=0, tiled=True) for a in (columns, d_values, b_values))
    dressed, spread_d, joined_b = own_pair(columns, d_all, b_all, amplitudes)

    state = None
    for lo, hi, piece in zip(marks, marks[1:], pieces):
        state = mirror_piece(lo, hi, columns, mirror_slot, piece, spread_d, joined_b, dressed, state)
    return state[1][None]


def solution(mesh):
    placed = (
        P(("pair", "fac"), None, None),
        P(("pair", "fac")),
        P("fac", None, None, None),
        P("fac", None),
        P("fac", None, None, None),
        P("fac", None),
    )
    return jax.shard_map(
        shards,
        mesh=mesh,
        in_specs=placed,
        out_specs=P(("pair", "fac"), None, None),
        check_vma=False,
    )
```

```python
import functools

import jax
import jax.numpy as jnp
from jax import lax
from jax.experimental import pallas as pl
from jax.experimental.pallas import tpu as pltpu
from jax.sharding import PartitionSpec as P

LANES = 128
BF16, F32 = jnp.bfloat16, jnp.float32
WHOLE = pl.BlockSpec(memory_space=pltpu.VMEM)
SCALARS = pl.BlockSpec(memory_space=pltpu.SMEM)
FAR = pl.BlockSpec(memory_space=pltpu.HBM)
VMEM_BYTES = 28 << 20


def params():
    return pltpu.CompilerParams(vmem_limit_bytes=VMEM_BYTES)


def aligned(start, size):
    return pl.ds(pl.multiple_of(start, size), size)


def strips_of(marks):
    return range(marks[0] // LANES * LANES, marks[-1], LANES)


def turn_kernel(marks, source, *rest):
    turned, strips, sems = rest[:-2], rest[-2], rest[-1]
    starts = strips_of(marks)
    copies = [
        pltpu.make_async_copy(source.at[0, :, lo : lo + LANES], strips.at[i], sems.at[i]) for i, lo in enumerate(starts)
    ]
    for copy in copies:
        copy.start()
    for i, lo in enumerate(starts):
        copies[i].wait()
        strip = strips[i].T
        for first, last, piece in zip(marks, marks[1:], turned):
            a, b = max(lo, first), min(lo + LANES, last)
            if a < b:
                piece[0, a - first : b - first, :] = strip[a - lo : b - lo, :]


def turn(amplitudes, marks):
    size = amplitudes.shape[1]
    count = len(strips_of(marks))
    return pl.pallas_call(
        functools.partial(turn_kernel, marks),
        in_specs=[FAR],
        out_specs=[WHOLE] * (len(marks) - 1),
        out_shape=[jax.ShapeDtypeStruct((1, b - a, size), BF16) for a, b in zip(marks, marks[1:])],
        scratch_shapes=[pltpu.VMEM((count, size, LANES), BF16), pltpu.SemaphoreType.DMA((count,))],
        compiler_params=params(),
        name="turn",
    )(amplitudes)


def spread_right(values, columns, side, spread):
    factors, blocks, width = values.shape[:3]
    spread[...] = jnp.zeros(spread.shape, BF16)

    def one(group, carry):
        for q in range(factors):
            for i in range(2):
                s = 2 * group + i
                row = i * LANES + (columns[q, side, s] % 2) * width
                spread[q, group, aligned(row, width), i * width : (i + 1) * width] = values[q, s].T
        return carry

    lax.fori_loop(0, blocks // 2, one, 0)


def join_left(values, joined):
    factors, blocks, width = values.shape[:3]

    def one(r, carry):
        for q in range(factors):
            joined[r, :, q * width : (q + 1) * width] = values[q, r]
        return carry

    lax.fori_loop(0, blocks, one, 0)


def apply_right(pick, lanes, spread, q, middle, first, rows):
    for g in range(spread.shape[1]):
        picked = jnp.concatenate([pick(lanes(q, 2 * g)), pick(lanes(q, 2 * g + 1))], axis=1)
        product = jnp.dot(picked, spread[q, g], preferred_element_type=F32)
        middle[q, pl.ds(first, rows), g * LANES : (g + 1) * LANES] = product.astype(BF16)


def apply_left(r, joined, starts, middle):
    factors, width = middle.shape[0], joined.shape[1]
    picked = [middle[q, aligned(starts(q, r), width), :] for q in range(factors)]
    return jnp.dot(joined[r], jnp.concatenate(picked, axis=0), preferred_element_type=F32)


class Plan:
    def __init__(self, factors, blocks, pieces):
        self.blocks = blocks
        self.lanes = 0
        self.rows = factors * blocks
        self.order = 2 * factors * blocks
        self.begin = self.order + blocks
        self.slot = self.begin + pieces + 1
        self.size = self.slot + 1


def make_plan(marks, plan, columns, slot, scalars):
    factors, blocks = columns.shape[0], columns.shape[2]

    def offsets(s, carry):
        for q in range(factors):
            scalars[plan.lanes + q * blocks + s] = columns[q, 0, s] // 2 * LANES
            scalars[plan.rows + q * blocks + s] = columns[q, 1, s] * (LANES // 2)
        return carry

    lax.fori_loop(0, blocks, offsets, 0)
    place = jnp.int32(0)
    for j, (lo, hi) in enumerate(zip(marks, marks[1:])):
        scalars[plan.begin + j] = place

        def one(r, place, lo=lo, hi=hi):
            last = columns[0, 1, r]
            for q in range(1, factors):
                last = jnp.maximum(last, columns[q, 1, r])
            here = jnp.logical_and(last >= lo, last < hi)

            @pl.when(here)
            def _():
                scalars[plan.order + place] = r

            return place + here.astype(jnp.int32)

        place = lax.fori_loop(0, blocks, one, place)
    scalars[plan.begin + len(marks) - 1] = place
    scalars[plan.slot] = slot[0]


def own_kernel(
    marks, plan, columns, slot, d_all, b_all, source, dressed, spread_d, joined_b, scalars, spread_b, joined_d, middle
):
    factors, blocks, width = d_all.shape[:3]
    size = source.shape[1]
    make_plan(marks, plan, columns, slot, scalars)
    spread_right(b_all, columns, 1, spread_b)
    join_left(d_all, joined_d)
    spread_right(d_all, columns, 0, spread_d)
    join_left(b_all, joined_b)
    step = min(256, size)

    def right(q, carry):
        for m in range(0, size, step):
            apply_right(
                lambda lane: source[0, m : m + step, aligned(lane, LANES)],
                lambda q, s: columns[q, 1, s] // 2 * LANES,
                spread_b,
                q,
                middle,
                m,
                step,
            )
        return carry

    def left(r, carry):
        block = apply_left(r, joined_d, lambda q, r: columns[q, 0, r] * width, middle)
        dressed[aligned(r * width, width), :] = block.astype(BF16)
        return carry

    lax.fori_loop(0, factors, right, 0)
    lax.fori_loop(0, blocks, left, 0)


def own_pair(marks, plan, columns, slot, d_all, b_all, amplitudes):
    factors, blocks, width = d_all.shape[:3]
    size = amplitudes.shape[1]
    spread = (factors, blocks // 2, 2 * LANES, LANES)
    joined = (blocks, width, factors * width)
    return pl.pallas_call(
        functools.partial(own_kernel, marks, plan),
        in_specs=[SCALARS, SCALARS, WHOLE, WHOLE, WHOLE],
        out_specs=[WHOLE, WHOLE, WHOLE, SCALARS],
        out_shape=[
            pltpu.VMEM((size, size), BF16),
            pltpu.VMEM(spread, BF16),
            pltpu.VMEM(joined, BF16),
            jax.ShapeDtypeStruct((plan.size,), jnp.int32),
        ],
        scratch_shapes=[
            pltpu.VMEM(spread, BF16),
            pltpu.VMEM(joined, BF16),
            pltpu.VMEM((factors, size, size), BF16),
        ],
        compiler_params=params(),
        name="own",
    )(columns, slot, d_all, b_all, amplitudes)


def finish_rows(begin, end, plan, scalars, joined_b, dressed, middle, out, ready, sems):
    blocks, width = joined_b.shape[:2]

    def leave(i):
        r = scalars[plan.order + i]
        return pltpu.make_async_copy(ready.at[r], out.at[aligned(r * width, width), :], sems.at[r])

    def left(i, carry):
        r = scalars[plan.order + i]
        mirrored = apply_left(r, joined_b, lambda q, r: scalars[plan.rows + q * blocks + r], middle)
        own = dressed[aligned(r * width, width), :].astype(F32)
        ready[r] = (own + mirrored.astype(BF16).astype(F32)).astype(BF16)
        leave(i).start()
        return carry

    def wait(i, carry):
        leave(i).wait()
        return carry

    lax.fori_loop(begin, end, left, 0)
    lax.fori_loop(begin, end, wait, 0)


def take_in(q, piece, first, plan, scalars, spread_d, middle, step):
    slot, blocks = scalars[plan.slot], 2 * spread_d.shape[1]
    for m in range(0, piece.shape[1], step):
        rows = min(step, piece.shape[1] - m)
        apply_right(
            lambda lane: piece[slot, m : m + rows, aligned(lane, LANES)],
            lambda q, s: scalars[plan.lanes + q * blocks + s],
            spread_d,
            q,
            middle,
            first + m,
            rows,
        )


def mirror_kernel(j, marks, plan, scalars, piece, spread_d, joined_b, dressed, *rest):
    middle, out, ready, sems = rest[-4:]

    for q in range(spread_d.shape[0]):
        take_in(q, piece, marks[j] * joined_b.shape[1], plan, scalars, spread_d, middle, piece.shape[1])
    begin, end = scalars[plan.begin + j], scalars[plan.begin + j + 1]
    finish_rows(begin, end, plan, scalars, joined_b, dressed, middle, out, ready, sems)


def mirror_piece(j, marks, plan, scalars, piece, spread_d, joined_b, dressed, state):
    size = dressed.shape[0]
    blocks, width = joined_b.shape[:2]
    kept = pltpu.VMEM((spread_d.shape[0], size, size), BF16)
    return pl.pallas_call(
        functools.partial(mirror_kernel, j, marks, plan),
        in_specs=[SCALARS] + [WHOLE] * 4 + [WHOLE, FAR][: len(state)],
        out_specs=[WHOLE, FAR],
        out_shape=[kept, jax.ShapeDtypeStruct((size, size), BF16)],
        scratch_shapes=[pltpu.VMEM((blocks, width, size), BF16), pltpu.SemaphoreType.DMA((blocks,))],
        input_output_aliases={5: 0, 6: 1} if state else {},
        compiler_params=params(),
        name="mirror",
    )(scalars, piece, spread_d, joined_b, dressed, *state)


def cuts(blocks):
    return [m * blocks // 16 for m in (0, 6, 12, 14, 15, 16)]


def later(arrays, *after):
    return lax.optimization_barrier((arrays, after))[0]


def shards(amplitudes, mirror_slot, d_values, d_cols, b_values, b_cols):
    pairs = lax.axis_size("pair")
    perm = [(i, (i + pairs // 2) % pairs) for i in range(pairs)]
    assert amplitudes.shape[0] == 1
    blocks, width = d_values.shape[1], d_values.shape[2]

    marks = cuts(blocks)
    plan = Plan(lax.axis_size("fac") * d_cols.shape[0], blocks, len(marks) - 1)
    amplitudes = pltpu.with_memory_space_constraint(amplitudes, pltpu.HBM)

    def send(j, after):
        lanes = [m * width for m in marks[j : j + 2]]
        return lax.ppermute(turn(later(amplitudes, after), lanes)[0], "pair", perm)

    def gather(array):
        return lax.all_gather(array, "fac", axis=0, tiled=True)

    head = turn(amplitudes, [m * width for m in marks[:2]])[0]
    pieces = [lax.ppermute(head, "pair", perm), send(1, head)]
    columns, d_values, b_values = later((jnp.stack([d_cols, b_cols], axis=1), d_values, b_values), head)
    columns = gather(columns)
    pieces.append(send(2, columns))
    d_all = gather(later(d_values, columns))
    pieces.append(send(3, d_all))
    b_all = gather(later(b_values, d_all))
    pieces.append(send(4, b_all))
    dressed, spread_d, joined_b, scalars = own_pair(marks, plan, columns, mirror_slot, d_all, b_all, amplitudes)

    state = ()
    for j, piece in enumerate(pieces):
        state = mirror_piece(j, marks, plan, scalars, piece, spread_d, joined_b, dressed, state)
    return state[1][None]


def solution(mesh):
    placed = (
        P(("pair", "fac"), None, None),
        P(("pair", "fac")),
        P("fac", None, None, None),
        P("fac", None),
        P("fac", None, None, None),
        P("fac", None),
    )
    return jax.shard_map(
        shards,
        mesh=mesh,
        in_specs=placed,
        out_specs=P(("pair", "fac"), None, None),
        check_vma=False,
    )
```

```python
import functools

import jax
import jax.numpy as jnp
from jax import lax
from jax.experimental import pallas as pl
from jax.experimental.pallas import tpu as pltpu
from jax.sharding import PartitionSpec as P

LANES = 128
BF16, F32 = jnp.bfloat16, jnp.float32
WHOLE = pl.BlockSpec(memory_space=pltpu.VMEM)
SCALARS = pl.BlockSpec(memory_space=pltpu.SMEM)
FAR = pl.BlockSpec(memory_space=pltpu.HBM)
VMEM_BYTES = 28 << 20


def params():
    return pltpu.CompilerParams(vmem_limit_bytes=VMEM_BYTES)


def aligned(start, size):
    return pl.ds(pl.multiple_of(start, size), size)


def strips_of(marks):
    return range(marks[0] // LANES * LANES, marks[-1], LANES)


def turn_kernel(marks, source, *rest):
    turned, strips, sems = rest[:-2], rest[-2], rest[-1]
    starts = strips_of(marks)
    copies = [
        pltpu.make_async_copy(source.at[0, :, lo : lo + LANES], strips.at[i], sems.at[i]) for i, lo in enumerate(starts)
    ]
    for copy in copies:
        copy.start()
    for i, lo in enumerate(starts):
        copies[i].wait()
        strip = strips[i].T
        for first, last, piece in zip(marks, marks[1:], turned):
            a, b = max(lo, first), min(lo + LANES, last)
            if a < b:
                piece[0, a - first : b - first, :] = strip[a - lo : b - lo, :]


def turn(amplitudes, marks):
    size = amplitudes.shape[1]
    count = len(strips_of(marks))
    return pl.pallas_call(
        functools.partial(turn_kernel, marks),
        in_specs=[FAR],
        out_specs=[WHOLE] * (len(marks) - 1),
        out_shape=[jax.ShapeDtypeStruct((1, b - a, size), BF16) for a, b in zip(marks, marks[1:])],
        scratch_shapes=[pltpu.VMEM((count, size, LANES), BF16), pltpu.SemaphoreType.DMA((count,))],
        compiler_params=params(),
        name="turn",
    )(amplitudes)


def pick_kernel(marks, columns, turned, place, *rest):
    pieces, order, tally = rest[:-2], rest[-2], rest[-1]
    factors, blocks = columns.shape[0], columns.shape[2]
    fixed, width = marks[1], turned.shape[1] // (blocks - marks[1])

    def clear(c, carry):
        tally[c] = 0
        place[c] = c
        return carry

    def count(r, carry):
        for q in range(factors):
            c = columns[q, 1, r]
            tally[c] = tally[c] + 1
        return carry

    def select(at, carry):
        def better(c, best):
            wins = tally[c] > best[0]
            return jnp.where(wins, tally[c], best[0]), jnp.where(wins, c, best[1])

        c = lax.fori_loop(fixed, blocks, better, (jnp.int32(-1), jnp.int32(fixed)))[1]
        tally[c] = -2
        place[c] = at
        order[at] = c
        return carry

    lax.fori_loop(0, blocks, clear, 0)
    lax.fori_loop(0, blocks, count, 0)
    lax.fori_loop(fixed, blocks, select, 0)
    for lo, hi, piece in zip(marks[1:], marks[2:], pieces):
        for at in range(lo, hi):
            source = aligned((order[at] - fixed) * width, width)
            piece[0, (at - lo) * width : (at - lo + 1) * width, :] = turned[0, source, :]


def pick(marks, columns, turned):
    blocks, size = columns.shape[2], turned.shape[2]
    rows = [(hi - lo) * turned.shape[1] // (blocks - marks[1]) for lo, hi in zip(marks[1:], marks[2:])]
    return pl.pallas_call(
        functools.partial(pick_kernel, marks),
        in_specs=[SCALARS, WHOLE],
        out_specs=[SCALARS] + [WHOLE] * len(rows),
        out_shape=[jax.ShapeDtypeStruct((blocks,), jnp.int32)]
        + [jax.ShapeDtypeStruct((1, n, size), BF16) for n in rows],
        scratch_shapes=[pltpu.SMEM((blocks,), jnp.int32), pltpu.SMEM((blocks,), jnp.int32)],
        compiler_params=params(),
        name="pick",
    )(columns, turned)


def spread_right(values, columns, side, spread):
    factors, blocks, width = values.shape[:3]
    spread[...] = jnp.zeros(spread.shape, BF16)

    def one(group, carry):
        for q in range(factors):
            for i in range(2):
                s = 2 * group + i
                row = i * LANES + (columns[q, side, s] % 2) * width
                spread[q, group, aligned(row, width), i * width : (i + 1) * width] = values[q, s].T
        return carry

    lax.fori_loop(0, blocks // 2, one, 0)


def join_left(values, joined):
    factors, blocks, width = values.shape[:3]

    def one(r, carry):
        for q in range(factors):
            joined[r, :, q * width : (q + 1) * width] = values[q, r]
        return carry

    lax.fori_loop(0, blocks, one, 0)


def apply_right(pick, lanes, spread, q, middle, first, rows):
    for g in range(spread.shape[1]):
        picked = jnp.concatenate([pick(lanes(q, 2 * g)), pick(lanes(q, 2 * g + 1))], axis=1)
        product = jnp.dot(picked, spread[q, g], preferred_element_type=F32)
        middle[q, pl.ds(first, rows), g * LANES : (g + 1) * LANES] = product.astype(BF16)


def apply_left(r, joined, starts, middle):
    factors, width = middle.shape[0], joined.shape[1]
    picked = [middle[q, aligned(starts(q, r), width), :] for q in range(factors)]
    return jnp.dot(joined[r], jnp.concatenate(picked, axis=0), preferred_element_type=F32)


class Plan:
    def __init__(self, factors, blocks, pieces):
        self.blocks = blocks
        self.lanes = 0
        self.rows = factors * blocks
        self.order = 2 * factors * blocks
        self.begin = self.order + blocks
        self.slot = self.begin + pieces + 1
        self.uses = self.slot + 1
        self.size = self.uses + pieces * factors


def make_plan(marks, plan, columns, place, slot, scalars):
    factors, blocks = columns.shape[0], columns.shape[2]
    spans = list(zip(marks, marks[1:]))

    def offsets(s, uses):
        for q in range(factors):
            at = place[columns[q, 1, s]]
            scalars[plan.lanes + q * blocks + s] = columns[q, 0, s] // 2 * LANES
            scalars[plan.rows + q * blocks + s] = at * (LANES // 2)
            here = [jnp.logical_and(at >= lo, at < hi).astype(jnp.int32) for lo, hi in spans]
            uses = [n + here[i - q * len(spans)] if i // len(spans) == q else n for i, n in enumerate(uses)]
        return uses

    uses = lax.fori_loop(0, blocks, offsets, [jnp.int32(0)] * (factors * len(spans)))
    for i, n in enumerate(uses):
        scalars[plan.uses + i] = n
    found = jnp.int32(0)
    for j, (lo, hi) in enumerate(spans):
        scalars[plan.begin + j] = found

        def one(r, found, lo=lo, hi=hi):
            last = place[columns[0, 1, r]]
            for q in range(1, factors):
                last = jnp.maximum(last, place[columns[q, 1, r]])
            here = jnp.logical_and(last >= lo, last < hi)

            @pl.when(here)
            def _():
                scalars[plan.order + found] = r

            return found + here.astype(jnp.int32)

        found = lax.fori_loop(0, blocks, one, found)
    scalars[plan.begin + len(spans)] = found
    scalars[plan.slot] = slot[0]


def own_kernel(
    marks,
    plan,
    columns,
    place,
    slot,
    d_all,
    b_all,
    source,
    dressed,
    spread_d,
    joined_b,
    scalars,
    spread_b,
    joined_d,
    middle,
):
    factors, blocks, width = d_all.shape[:3]
    size = source.shape[1]
    make_plan(marks, plan, columns, place, slot, scalars)
    spread_right(b_all, columns, 1, spread_b)
    join_left(d_all, joined_d)
    spread_right(d_all, columns, 0, spread_d)
    join_left(b_all, joined_b)
    step = min(256, size)

    def right(q, carry):
        for m in range(0, size, step):
            apply_right(
                lambda lane: source[0, m : m + step, aligned(lane, LANES)],
                lambda q, s: columns[q, 1, s] // 2 * LANES,
                spread_b,
                q,
                middle,
                m,
                step,
            )
        return carry

    def left(r, carry):
        block = apply_left(r, joined_d, lambda q, r: columns[q, 0, r] * width, middle)
        dressed[aligned(r * width, width), :] = block.astype(BF16)
        return carry

    lax.fori_loop(0, factors, right, 0)
    lax.fori_loop(0, blocks, left, 0)


def own_pair(marks, plan, columns, place, slot, d_all, b_all, amplitudes):
    factors, blocks, width = d_all.shape[:3]
    size = amplitudes.shape[1]
    spread = (factors, blocks // 2, 2 * LANES, LANES)
    joined = (blocks, width, factors * width)
    return pl.pallas_call(
        functools.partial(own_kernel, marks, plan),
        in_specs=[SCALARS, SCALARS, SCALARS, WHOLE, WHOLE, WHOLE],
        out_specs=[WHOLE, WHOLE, WHOLE, SCALARS],
        out_shape=[
            pltpu.VMEM((size, size), BF16),
            pltpu.VMEM(spread, BF16),
            pltpu.VMEM(joined, BF16),
            jax.ShapeDtypeStruct((plan.size,), jnp.int32),
        ],
        scratch_shapes=[
            pltpu.VMEM(spread, BF16),
            pltpu.VMEM(joined, BF16),
            pltpu.VMEM((factors, size, size), BF16),
        ],
        compiler_params=params(),
        name="own",
    )(columns, place, slot, d_all, b_all, amplitudes)


def finish_rows(begin, end, plan, scalars, joined_b, dressed, middle, out, ready, sems):
    blocks, width = joined_b.shape[:2]

    def leave(i):
        r = scalars[plan.order + i]
        return pltpu.make_async_copy(ready.at[r], out.at[aligned(r * width, width), :], sems.at[r])

    def left(i, carry):
        r = scalars[plan.order + i]
        mirrored = apply_left(r, joined_b, lambda q, r: scalars[plan.rows + q * blocks + r], middle)
        own = dressed[aligned(r * width, width), :].astype(F32)
        ready[r] = (own + mirrored.astype(BF16).astype(F32)).astype(BF16)
        leave(i).start()
        return carry

    def wait(i, carry):
        leave(i).wait()
        return carry

    lax.fori_loop(begin, end, left, 0)
    lax.fori_loop(begin, end, wait, 0)


def take_in(q, piece, first, plan, scalars, spread_d, middle, step):
    slot, blocks = scalars[plan.slot], 2 * spread_d.shape[1]
    for m in range(0, piece.shape[1], step):
        rows = min(step, piece.shape[1] - m)
        apply_right(
            lambda lane: piece[slot, m : m + rows, aligned(lane, LANES)],
            lambda q, s: scalars[plan.lanes + q * blocks + s],
            spread_d,
            q,
            middle,
            first + m,
            rows,
        )


def mirror_kernel(j, marks, plan, scalars, piece, spread_d, joined_b, dressed, *rest):
    middle, out, ready, sems = rest[-4:]

    factors, width = spread_d.shape[0], joined_b.shape[1]
    for q in range(factors):

        @pl.when(scalars[plan.uses + q * (len(marks) - 1) + j] > 0)
        def _(q=q):
            take_in(q, piece, marks[j] * width, plan, scalars, spread_d, middle, piece.shape[1])

    begin, end = scalars[plan.begin + j], scalars[plan.begin + j + 1]
    finish_rows(begin, end, plan, scalars, joined_b, dressed, middle, out, ready, sems)


def mirror_piece(j, marks, plan, scalars, piece, spread_d, joined_b, dressed, state):
    size = dressed.shape[0]
    blocks, width = joined_b.shape[:2]
    kept = pltpu.VMEM((spread_d.shape[0], size, size), BF16)
    return pl.pallas_call(
        functools.partial(mirror_kernel, j, marks, plan),
        in_specs=[SCALARS] + [WHOLE] * 4 + [WHOLE, FAR][: len(state)],
        out_specs=[WHOLE, FAR],
        out_shape=[kept, jax.ShapeDtypeStruct((size, size), BF16)],
        scratch_shapes=[pltpu.VMEM((blocks, width, size), BF16), pltpu.SemaphoreType.DMA((blocks,))],
        input_output_aliases={5: 0, 6: 1} if state else {},
        compiler_params=params(),
        name="mirror",
    )(scalars, piece, spread_d, joined_b, dressed, *state)


def cuts(blocks):
    return [m * blocks // 16 for m in (0, 6, 12, 14, 15, 16)]


def later(arrays, *after):
    return lax.optimization_barrier((arrays, after))[0]


def shards(amplitudes, mirror_slot, d_values, d_cols, b_values, b_cols):
    pairs = lax.axis_size("pair")
    perm = [(i, (i + pairs // 2) % pairs) for i in range(pairs)]
    assert amplitudes.shape[0] == 1
    blocks, width = d_values.shape[1], d_values.shape[2]

    marks = cuts(blocks)
    plan = Plan(lax.axis_size("fac") * d_cols.shape[0], blocks, len(marks) - 1)
    amplitudes = pltpu.with_memory_space_constraint(amplitudes, pltpu.HBM)

    def send(piece):
        return lax.ppermute(piece, "pair", perm)

    def gather(array):
        return lax.all_gather(array, "fac", axis=0, tiled=True)

    lanes = [m * width for m in marks]
    head = turn(amplitudes, lanes[:2])[0]
    pieces = [send(head)]
    rest = turn(later(amplitudes, head), [lanes[1], lanes[-1]])[0]
    columns = gather(later(jnp.stack([d_cols, b_cols], axis=1), rest))
    place, *picked = pick(marks, columns, rest)
    pieces.append(send(picked[0]))
    d_all = gather(later(d_values, picked))
    pieces.append(send(later(picked[1], d_all)))
    b_all = gather(later(b_values, d_all))
    pieces.append(send(later(picked[2], b_all)))
    own = own_pair(marks, plan, columns, place, mirror_slot, d_all, b_all, amplitudes)
    dressed, spread_d, joined_b, scalars = own
    pieces.append(send(later(picked[3], dressed)))

    state = ()
    for j, piece in enumerate(pieces):
        state = mirror_piece(j, marks, plan, scalars, piece, spread_d, joined_b, dressed, state)
    return state[1][None]


def solution(mesh):
    placed = (
        P(("pair", "fac"), None, None),
        P(("pair", "fac")),
        P("fac", None, None, None),
        P("fac", None),
        P("fac", None, None, None),
        P("fac", None),
    )
    return jax.shard_map(
        shards,
        mesh=mesh,
        in_specs=placed,
        out_specs=P(("pair", "fac"), None, None),
        check_vma=False,
    )
```

```python
import functools

import jax
import jax.numpy as jnp
from jax import lax
from jax.experimental import pallas as pl
from jax.experimental.pallas import tpu as pltpu
from jax.sharding import PartitionSpec as P

LANES = 128
BF16, F32 = jnp.bfloat16, jnp.float32
WHOLE = pl.BlockSpec(memory_space=pltpu.VMEM)
SCALARS = pl.BlockSpec(memory_space=pltpu.SMEM)
FAR = pl.BlockSpec(memory_space=pltpu.HBM)
VMEM_BYTES = 28 << 20


def params():
    return pltpu.CompilerParams(vmem_limit_bytes=VMEM_BYTES)


def aligned(start, size):
    return pl.ds(pl.multiple_of(start, size), size)


def strips_of(marks):
    return range(marks[0] // LANES * LANES, marks[-1], LANES)


def turn_kernel(marks, source, *rest):
    turned, strips, sems = rest[:-2], rest[-2], rest[-1]
    starts = strips_of(marks)
    copies = [
        pltpu.make_async_copy(source.at[0, :, lo : lo + LANES], strips.at[i], sems.at[i]) for i, lo in enumerate(starts)
    ]
    for copy in copies:
        copy.start()
    for i, lo in enumerate(starts):
        copies[i].wait()
        strip = strips[i].T
        for first, last, piece in zip(marks, marks[1:], turned):
            a, b = max(lo, first), min(lo + LANES, last)
            if a < b:
                piece[0, a - first : b - first, :] = strip[a - lo : b - lo, :]


def turn(amplitudes, marks):
    size = amplitudes.shape[1]
    count = len(strips_of(marks))
    return pl.pallas_call(
        functools.partial(turn_kernel, marks),
        in_specs=[FAR],
        out_specs=[WHOLE] * (len(marks) - 1),
        out_shape=[jax.ShapeDtypeStruct((1, b - a, size), BF16) for a, b in zip(marks, marks[1:])],
        scratch_shapes=[pltpu.VMEM((count, size, LANES), BF16), pltpu.SemaphoreType.DMA((count,))],
        compiler_params=params(),
        name="turn",
    )(amplitudes)


class Layout:
    def __init__(self, blocks):
        self.blocks = blocks
        self.place = 0
        self.used = blocks
        self.slot = 2 * blocks + 1
        self.block = self.slot + blocks * blocks
        self.size = self.block + blocks * blocks


def swap_halves(tile):
    half = tile.shape[1] // 2
    return jnp.concatenate([tile[:, half:], tile[:, :half]], axis=1)


def join_halves(low, low_swapped, high, high_swapped):
    low = jnp.where(low_swapped, swap_halves(low), low)
    high = jnp.where(high_swapped, swap_halves(high), high)
    lane = lax.broadcasted_iota(jnp.int32, low.shape, 1)
    return jnp.where(lane < low.shape[1] // 2, low, high)


def pack(start, piece, fixed, layout, scalars, turned):
    blocks = layout.blocks
    width = turned.shape[1] // (blocks - fixed)
    tiles = piece.shape[2] // LANES
    group = 4 if tiles % 4 == 0 else 2 if tiles % 2 == 0 else 1

    def half(slot):
        at = scalars[layout.block + slot]
        row, k = at // blocks, at % blocks
        return turned[0, aligned(row * width, width), aligned(k // 2 * LANES, LANES)], k % 2

    def fill(i, carry):
        for n in range(group):
            tile = i * group + n
            low, k_low = half(start + 2 * tile)
            high, k_high = half(start + 2 * tile + 1)
            piece[0, :, aligned(tile * LANES, LANES)] = join_halves(low, k_low == 1, high, k_high == 0)
        return carry

    lax.fori_loop(0, tiles // group, fill, 0)


def pack_kernel(starts, fixed, layout, scalars, turned, *pieces):
    for start, piece in zip(starts, pieces):
        pack(start, piece, fixed, layout, scalars, turned)


def pick_kernel(starts, fixed, layout, columns, turned, scalars, *rest):
    pieces, tally = rest[:-1], rest[-1]
    factors, blocks = columns.shape[0], columns.shape[2]

    def clear(c, carry):
        tally[c] = 0
        scalars[layout.place + c] = c
        scalars[layout.used + c] = 0
        for k in range(blocks):
            scalars[layout.block + c * blocks + k] = 0
        return carry

    def count(r, masks):
        left, right = [], []
        for q in range(factors):
            c = columns[q, 1, r]
            tally[c] = tally[c] + 1
            left.append(masks[0][q] | jnp.left_shift(1, c))
            right.append(masks[1][q] | jnp.left_shift(1, columns[q, 0, r]))
        return left, right

    lax.fori_loop(0, blocks, clear, 0)
    none = [jnp.int32(0)] * factors
    left, right = lax.fori_loop(0, blocks, count, (none, none))

    def select(at, used):
        def better(c, best):
            wins = tally[c] > best[0]
            return jnp.where(wins, tally[c], best[0]), jnp.where(wins, c, best[1])

        c = lax.fori_loop(fixed, blocks, better, (jnp.int32(-1), jnp.int32(fixed)))[1]
        tally[c] = -2
        scalars[layout.place + c] = at
        scalars[layout.used + at] = used
        read = jnp.int32(0)
        for q in range(factors):
            read = read | jnp.where(jnp.right_shift(left[q], c) & 1 == 1, right[q], 0)
        for k in range(blocks):
            bit = jnp.right_shift(read, k) & 1
            scalars[layout.block + used] = (c - fixed) * blocks + k
            scalars[layout.slot + at * blocks + k] = jnp.where(bit == 1, used, 0)
            used = used + bit
        return used

    scalars[layout.used + blocks] = lax.fori_loop(fixed, blocks, select, jnp.int32(0))

    pack_kernel(starts, fixed, layout, scalars, turned, *pieces)


def pack_pieces(given, spans, fixed, layout, turned):
    opening = given.ndim == 3
    blocks = layout.blocks
    width = turned.shape[1] // (blocks - fixed)
    shapes = [jax.ShapeDtypeStruct((1, width, (hi - lo) * width), BF16) for lo, hi in spans]
    kernel = functools.partial(pick_kernel if opening else pack_kernel, [lo for lo, _ in spans], fixed, layout)
    return pl.pallas_call(
        kernel,
        in_specs=[SCALARS, WHOLE],
        out_specs=[SCALARS] * opening + [WHOLE] * len(spans),
        out_shape=[jax.ShapeDtypeStruct((layout.size,), jnp.int32)] * opening + shapes,
        scratch_shapes=[pltpu.SMEM((blocks,), jnp.int32)] * opening,
        compiler_params=params(),
        name="pack",
    )(given, turned)


def spread_right(values, columns, side, spread):
    factors, blocks, width = values.shape[:3]
    spread[...] = jnp.zeros(spread.shape, BF16)

    def one(group, carry):
        for q in range(factors):
            for i in range(2):
                s = 2 * group + i
                row = i * LANES + (columns[q, side, s] % 2) * width
                spread[q, group, aligned(row, width), i * width : (i + 1) * width] = values[q, s].T
        return carry

    lax.fori_loop(0, blocks // 2, one, 0)


def join_left(values, joined):
    factors, blocks, width = values.shape[:3]

    def one(r, carry):
        for q in range(factors):
            joined[r, :, q * width : (q + 1) * width] = values[q, r]
        return carry

    lax.fori_loop(0, blocks, one, 0)


def apply_right(pick, lanes, spread, q, middle, first, rows):
    for g in range(spread.shape[1]):
        picked = jnp.concatenate([pick(lanes(q, 2 * g)), pick(lanes(q, 2 * g + 1))], axis=1)
        product = jnp.dot(picked, spread[q, g], preferred_element_type=F32)
        middle[q, pl.ds(first, rows), g * LANES : (g + 1) * LANES] = product.astype(BF16)


def apply_left(r, joined, starts, middle):
    factors, width = middle.shape[0], joined.shape[1]
    picked = [middle[q, aligned(starts(q, r), width), :] for q in range(factors)]
    return jnp.dot(joined[r], jnp.concatenate(picked, axis=0), preferred_element_type=F32)


class Plan:
    def __init__(self, factors, blocks, pieces):
        self.blocks = blocks
        self.lanes = 0
        self.rows = factors * blocks
        self.uses = 2 * factors * blocks
        self.slot = 3 * factors * blocks
        self.whole = self.slot + blocks * blocks
        self.order = self.whole + pieces
        self.begin = self.order + blocks
        self.mirror = self.begin + pieces + 1
        self.size = self.mirror + 1


def make_plan(fixed, ends, plan, layout, columns, packing, slot, scalars):
    factors, blocks = columns.shape[0], columns.shape[2]

    def clear(i, carry):
        scalars[plan.uses + i] = 0
        return carry

    def offsets(s, carry):
        for q in range(factors):
            at = packing[layout.place + columns[q, 1, s]]
            scalars[plan.lanes + q * blocks + s] = columns[q, 0, s] // 2 * LANES
            scalars[plan.rows + q * blocks + s] = at * (LANES // 2)
            use = plan.uses + q * blocks + at
            scalars[use] = scalars[use] + 1
        return carry

    def copy(i, carry):
        scalars[plan.slot + i] = packing[layout.slot + i]
        return carry

    lax.fori_loop(0, factors * blocks, clear, 0)
    lax.fori_loop(0, blocks, offsets, 0)
    lax.fori_loop(fixed * blocks, blocks * blocks, copy, 0)
    found, low = jnp.int32(0), jnp.int32(0)
    for j, end in enumerate(ends):

        def ready(at, n, end=end):
            return n + (jnp.minimum(packing[layout.used + at + 1], ends[-1]) <= end).astype(jnp.int32)

        high = lax.fori_loop(fixed, blocks, ready, jnp.int32(fixed)) if j else jnp.int32(fixed)
        scalars[plan.whole + j] = high
        scalars[plan.begin + j] = found

        def one(r, found, low=low, high=high):
            last = packing[layout.place + columns[0, 1, r]]
            for q in range(1, factors):
                last = jnp.maximum(last, packing[layout.place + columns[q, 1, r]])
            here = jnp.logical_and(last >= low, last < high)

            @pl.when(here)
            def _():
                scalars[plan.order + found] = r

            return found + here.astype(jnp.int32)

        found, low = lax.fori_loop(0, blocks, one, found), high
    scalars[plan.begin + len(ends)] = found
    scalars[plan.mirror] = slot[0]


def own_kernel(
    fixed,
    ends,
    plan,
    layout,
    columns,
    packing,
    slot,
    d_all,
    b_all,
    source,
    dressed,
    spread_d,
    joined_b,
    scalars,
    spread_b,
    joined_d,
    middle,
):
    factors, blocks, width = d_all.shape[:3]
    size = source.shape[1]
    make_plan(fixed, ends, plan, layout, columns, packing, slot, scalars)
    spread_right(b_all, columns, 1, spread_b)
    join_left(d_all, joined_d)
    spread_right(d_all, columns, 0, spread_d)
    join_left(b_all, joined_b)
    step = min(256, size)

    def right(q, carry):
        for m in range(0, size, step):
            apply_right(
                lambda lane: source[0, m : m + step, aligned(lane, LANES)],
                lambda q, s: columns[q, 1, s] // 2 * LANES,
                spread_b,
                q,
                middle,
                m,
                step,
            )
        return carry

    def left(r, carry):
        block = apply_left(r, joined_d, lambda q, r: columns[q, 0, r] * width, middle)
        dressed[aligned(r * width, width), :] = block.astype(BF16)
        return carry

    lax.fori_loop(0, factors, right, 0)
    lax.fori_loop(0, blocks, left, 0)


def own_pair(fixed, ends, plan, layout, columns, packing, slot, d_all, b_all, amplitudes):
    factors, blocks, width = d_all.shape[:3]
    size = amplitudes.shape[1]
    spread = (factors, blocks // 2, 2 * LANES, LANES)
    joined = (blocks, width, factors * width)
    return pl.pallas_call(
        functools.partial(own_kernel, fixed, ends, plan, layout),
        in_specs=[SCALARS, SCALARS, SCALARS, WHOLE, WHOLE, WHOLE],
        out_specs=[WHOLE, WHOLE, WHOLE, SCALARS],
        out_shape=[
            pltpu.VMEM((size, size), BF16),
            pltpu.VMEM(spread, BF16),
            pltpu.VMEM(joined, BF16),
            jax.ShapeDtypeStruct((plan.size,), jnp.int32),
        ],
        scratch_shapes=[
            pltpu.VMEM(spread, BF16),
            pltpu.VMEM(joined, BF16),
            pltpu.VMEM((factors, size, size), BF16),
        ],
        compiler_params=params(),
        name="own",
    )(columns, packing, slot, d_all, b_all, amplitudes)


def finish_rows(begin, end, plan, scalars, joined_b, dressed, middle, out, ready, sems):
    blocks, width = joined_b.shape[:2]

    def leave(i):
        r = scalars[plan.order + i]
        return pltpu.make_async_copy(ready.at[r], out.at[aligned(r * width, width), :], sems.at[r])

    def left(i, carry):
        r = scalars[plan.order + i]
        mirrored = apply_left(r, joined_b, lambda q, r: scalars[plan.rows + q * blocks + r], middle)
        own = dressed[aligned(r * width, width), :].astype(F32)
        ready[r] = (own + mirrored.astype(BF16).astype(F32)).astype(BF16)
        leave(i).start()
        return carry

    def wait(i, carry):
        leave(i).wait()
        return carry

    lax.fori_loop(begin, end, left, 0)
    lax.fori_loop(begin, end, wait, 0)


def opening_kernel(plan, scalars, piece, spread_d, joined_b, dressed, middle, packed, out, ready, sems):
    slot, blocks = scalars[plan.mirror], joined_b.shape[0]
    rows = piece.shape[1]
    packed[...] = jnp.zeros(packed.shape, BF16)
    for q in range(spread_d.shape[0]):
        apply_right(
            lambda lane: piece[slot, :, aligned(lane, LANES)],
            lambda q, s: scalars[plan.lanes + q * blocks + s],
            spread_d,
            q,
            middle,
            0,
            rows,
        )
    end = scalars[plan.begin + 1]
    finish_rows(0, end, plan, scalars, joined_b, dressed, middle, out, ready, sems)


def packed_kernel(j, starts, plan, scalars, spread_d, joined_b, dressed, *rest):
    pieces, rest = rest[: len(starts)], rest[len(starts) + 3 :]
    middle, packed, out, row, ready, sems = rest
    slot, factors = scalars[plan.mirror], spread_d.shape[0]
    blocks, width = joined_b.shape[:2]
    for start, piece in zip(starts, pieces):
        for lane in range(0, piece.shape[2], LANES):
            packed[:, start * width + lane : start * width + lane + LANES] = piece[slot, :, lane : lane + LANES]

    fixed = scalars[plan.whole]
    before, after = scalars[plan.whole + j - 1], scalars[plan.whole + j]

    def take(i, carry):
        first = jnp.maximum(jnp.minimum(before + 2 * i, after - 2), fixed)
        for n in range(2):
            for k in range(0, blocks, 2):
                low, high = (scalars[plan.slot + (first + n) * blocks + k + i] for i in range(2))
                tiles = [packed[:, aligned(slot // 2 * LANES, LANES)] for slot in (low, high)]
                tile = join_halves(tiles[0], low % 2 == 1, tiles[1], high % 2 == 0)
                row[n * width : (n + 1) * width, k * width : (k + 2) * width] = tile
        for q in range(factors):
            uses = plan.uses + q * blocks + first

            @pl.when(scalars[uses] + scalars[uses + 1] > 0)
            def _(q=q):
                apply_right(
                    lambda lane: row[:, aligned(lane, LANES)],
                    lambda q, s: scalars[plan.lanes + q * blocks + s],
                    spread_d,
                    q,
                    middle,
                    pl.multiple_of(first * width, width),
                    2 * width,
                )

        return carry

    lax.fori_loop(0, (after - before + 1) // 2, take, 0)
    begin, end = scalars[plan.begin + j], scalars[plan.begin + j + 1]
    finish_rows(begin, end, plan, scalars, joined_b, dressed, middle, out, ready, sems)


def mirror_piece(j, starts, slots, plan, scalars, pieces, spread_d, joined_b, dressed, state):
    size, (blocks, width) = dressed.shape[0], joined_b.shape[:2]
    shapes = [
        pltpu.VMEM((spread_d.shape[0], size, size), BF16),
        pltpu.VMEM((width, slots * width), BF16),
        jax.ShapeDtypeStruct((size, size), BF16),
    ]
    scratch = [pltpu.VMEM((blocks, width, size), BF16), pltpu.SemaphoreType.DMA((blocks,))]
    if j == 0:
        kernel, given = functools.partial(opening_kernel, plan), (scalars, *pieces, spread_d, joined_b, dressed)
    else:
        kernel, given = functools.partial(packed_kernel, j, starts, plan), (scalars, spread_d, joined_b, dressed, *pieces)
        scratch = [pltpu.VMEM((2 * width, size), BF16)] + scratch
    return pl.pallas_call(
        kernel,
        in_specs=[SCALARS] + [WHOLE] * (len(given) - 1) + [WHOLE, WHOLE, FAR][: len(state)],
        out_specs=[WHOLE, WHOLE, FAR],
        out_shape=shapes,
        scratch_shapes=scratch,
        input_output_aliases={len(given) + i: i for i in range(len(state))},
        compiler_params=params(),
        name="mirror",
    )(*given, *state)


def cuts(blocks):
    fixed = blocks // 4
    slots = (blocks - fixed) * blocks
    return fixed, [slots * m // 192 // 2 * 2 for m in (0, 64, 128, 160, 180)], slots


def later(arrays, *after):
    return lax.optimization_barrier((arrays, after))[0]


def shards(amplitudes, mirror_slot, d_values, d_cols, b_values, b_cols):
    pairs = lax.axis_size("pair")
    perm = [(i, (i + pairs // 2) % pairs) for i in range(pairs)]
    assert amplitudes.shape[0] == 1
    blocks, width = d_values.shape[1], d_values.shape[2]

    fixed, marks, slots = cuts(blocks)
    ends = [0] + marks[1:]
    layout = Layout(blocks)
    plan = Plan(lax.axis_size("fac") * d_cols.shape[0], blocks, len(ends))
    amplitudes = pltpu.with_memory_space_constraint(amplitudes, pltpu.HBM)

    def send(piece):
        return lax.ppermute(piece, "pair", perm)

    def gather(array):
        return lax.all_gather(array, "fac", axis=0, tiled=True)

    head = turn(amplitudes, [0, fixed * width])[0]
    pieces = [[send(head)]]
    rest = turn(later(amplitudes, head), [fixed * width, blocks * width])[0]
    columns = gather(later(jnp.stack([d_cols, b_cols], axis=1), rest))
    spans = list(zip(marks, marks[1:]))
    packing, picked, over = pack_pieces(columns, [spans[0], (marks[-1], slots)], fixed, layout, rest)
    over = lax.cond(packing[layout.used + blocks] > marks[-1], send, lambda piece: piece, over)
    picked = later(picked, over)
    pieces.append([send(picked), over])
    picked = [picked, *pack_pieces(later(packing, picked), spans[1:], fixed, layout, rest)]
    d_all = gather(later(d_values, picked))
    pieces.append([send(later(picked[1], d_all))])
    b_all = gather(later(b_values, d_all))
    pieces.append([send(later(picked[2], b_all))])
    own = own_pair(fixed, ends, plan, layout, columns, packing, mirror_slot, d_all, b_all, amplitudes)
    dressed, spread_d, joined_b, scalars = own
    pieces.append([send(later(picked[3], dressed))])

    state = ()
    for j, arrived in enumerate(pieces):
        starts = [] if j == 0 else [marks[j - 1], marks[-1]][: len(arrived)]
        state = mirror_piece(j, starts, slots, plan, scalars, arrived, spread_d, joined_b, dressed, state)
    return state[2][None]


def solution(mesh):
    placed = (
        P(("pair", "fac"), None, None),
        P(("pair", "fac")),
        P("fac", None, None, None),
        P("fac", None),
        P("fac", None, None, None),
        P("fac", None),
    )
    return jax.shard_map(
        shards,
        mesh=mesh,
        in_specs=placed,
        out_specs=P(("pair", "fac"), None, None),
        check_vma=False,
    )
```

```python
import functools

import jax
import jax.numpy as jnp
from jax import lax
from jax.experimental import pallas as pl
from jax.experimental.pallas import tpu as pltpu
from jax.sharding import PartitionSpec as P

LANES = 128
BF16, F32 = jnp.bfloat16, jnp.float32
WHOLE = pl.BlockSpec(memory_space=pltpu.VMEM)
SCALARS = pl.BlockSpec(memory_space=pltpu.SMEM)
FAR = pl.BlockSpec(memory_space=pltpu.HBM)
VMEM_BYTES = 28 << 20


def params():
    return pltpu.CompilerParams(vmem_limit_bytes=VMEM_BYTES)


def aligned(start, size):
    return pl.ds(pl.multiple_of(start, size), size)


def strips_of(marks):
    return range(marks[0] // LANES * LANES, marks[-1], LANES)


def turn_kernel(marks, source, *rest):
    turned, strips, sems = rest[:-2], rest[-2], rest[-1]
    starts = strips_of(marks)
    copies = [
        pltpu.make_async_copy(source.at[0, :, lo : lo + LANES], strips.at[i], sems.at[i]) for i, lo in enumerate(starts)
    ]
    for copy in copies:
        copy.start()
    for i, lo in enumerate(starts):
        copies[i].wait()
        strip = strips[i].T
        for first, last, piece in zip(marks, marks[1:], turned):
            a, b = max(lo, first), min(lo + LANES, last)
            if a < b:
                piece[0, a - first : b - first, :] = strip[a - lo : b - lo, :]


def turn(amplitudes, marks):
    size = amplitudes.shape[1]
    count = len(strips_of(marks))
    return pl.pallas_call(
        functools.partial(turn_kernel, marks),
        in_specs=[FAR],
        out_specs=[WHOLE] * (len(marks) - 1),
        out_shape=[jax.ShapeDtypeStruct((1, b - a, size), BF16) for a, b in zip(marks, marks[1:])],
        scratch_shapes=[pltpu.VMEM((count, size, LANES), BF16), pltpu.SemaphoreType.DMA((count,))],
        compiler_params=params(),
        name="turn",
    )(amplitudes)


class Layout:
    def __init__(self, blocks):
        self.blocks = blocks
        self.place = 0
        self.used = blocks
        self.slot = 2 * blocks + 1
        self.block = self.slot + blocks * blocks
        self.size = self.block + blocks * blocks


def swap_halves(tile):
    half = tile.shape[1] // 2
    return jnp.concatenate([tile[:, half:], tile[:, :half]], axis=1)


def join_halves(low, low_swapped, high, high_swapped):
    low = jnp.where(low_swapped, swap_halves(low), low)
    high = jnp.where(high_swapped, swap_halves(high), high)
    lane = lax.broadcasted_iota(jnp.int32, low.shape, 1)
    return jnp.where(lane < low.shape[1] // 2, low, high)


def pack(start, piece, fixed, layout, scalars, turned):
    blocks = layout.blocks
    width = turned.shape[1] // (blocks - fixed)
    tiles = piece.shape[2] // LANES
    group = 4 if tiles % 4 == 0 else 2 if tiles % 2 == 0 else 1

    def half(slot):
        at = scalars[layout.block + slot]
        row, k = at // blocks, at % blocks
        return turned[0, aligned(row * width, width), aligned(k // 2 * LANES, LANES)], k % 2

    def fill(i, carry):
        for n in range(group):
            tile = i * group + n
            low, k_low = half(start + 2 * tile)
            high, k_high = half(start + 2 * tile + 1)
            piece[0, :, aligned(tile * LANES, LANES)] = join_halves(low, k_low == 1, high, k_high == 0)
        return carry

    lax.fori_loop(0, tiles // group, fill, 0)


def pack_kernel(starts, fixed, layout, scalars, turned, *pieces):
    for start, piece in zip(starts, pieces):
        pack(start, piece, fixed, layout, scalars, turned)


def pick_kernel(starts, fixed, layout, columns, turned, scalars, *rest):
    pieces, tally = rest[:-1], rest[-1]
    factors, blocks = columns.shape[0], columns.shape[2]

    def clear(c, carry):
        tally[c] = 0
        scalars[layout.place + c] = c
        scalars[layout.used + c] = 0
        for k in range(blocks):
            scalars[layout.block + c * blocks + k] = 0
        return carry

    def count(r, masks):
        left, right = [], []
        for q in range(factors):
            c = columns[q, 1, r]
            tally[c] = tally[c] + 1
            left.append(masks[0][q] | jnp.left_shift(1, c))
            right.append(masks[1][q] | jnp.left_shift(1, columns[q, 0, r]))
        return left, right

    lax.fori_loop(0, blocks, clear, 0)
    none = [jnp.int32(0)] * factors
    left, right = lax.fori_loop(0, blocks, count, (none, none))

    def select(at, used):
        def better(c, best):
            wins = tally[c] > best[0]
            return jnp.where(wins, tally[c], best[0]), jnp.where(wins, c, best[1])

        c = lax.fori_loop(fixed, blocks, better, (jnp.int32(-1), jnp.int32(fixed)))[1]
        tally[c] = -2
        scalars[layout.place + c] = at
        scalars[layout.used + at] = used
        read = jnp.int32(0)
        for q in range(factors):
            read = read | jnp.where(jnp.right_shift(left[q], c) & 1 == 1, right[q], 0)
        for k in range(blocks):
            bit = jnp.right_shift(read, k) & 1
            scalars[layout.block + used] = (c - fixed) * blocks + k
            scalars[layout.slot + at * blocks + k] = jnp.where(bit == 1, used, 0)
            used = used + bit
        return used

    scalars[layout.used + blocks] = lax.fori_loop(fixed, blocks, select, jnp.int32(0))

    pack_kernel(starts, fixed, layout, scalars, turned, *pieces)


def pack_pieces(given, spans, fixed, layout, turned):
    opening = given.ndim == 3
    blocks = layout.blocks
    width = turned.shape[1] // (blocks - fixed)
    shapes = [jax.ShapeDtypeStruct((1, width, (hi - lo) * width), BF16) for lo, hi in spans]
    kernel = functools.partial(pick_kernel if opening else pack_kernel, [lo for lo, _ in spans], fixed, layout)
    return pl.pallas_call(
        kernel,
        in_specs=[SCALARS, WHOLE],
        out_specs=[SCALARS] * opening + [WHOLE] * len(spans),
        out_shape=[jax.ShapeDtypeStruct((layout.size,), jnp.int32)] * opening + shapes,
        scratch_shapes=[pltpu.SMEM((blocks,), jnp.int32)] * opening,
        compiler_params=params(),
        name="pack",
    )(given, turned)


def spread_right(values, columns, side, spread):
    factors, blocks, width = values.shape[:3]
    spread[...] = jnp.zeros(spread.shape, BF16)

    def one(group, carry):
        for q in range(factors):
            for i in range(2):
                s = 2 * group + i
                row = i * LANES + (columns[q, side, s] % 2) * width
                spread[q, group, aligned(row, width), i * width : (i + 1) * width] = values[q, s].T
        return carry

    lax.fori_loop(0, blocks // 2, one, 0)


def join_left(values, joined):
    factors, blocks, width = values.shape[:3]

    def one(r, carry):
        for q in range(factors):
            joined[r, :, q * width : (q + 1) * width] = values[q, r]
        return carry

    lax.fori_loop(0, blocks, one, 0)


def apply_right(pick, lanes, spread, q, middle, first, rows):
    for g in range(spread.shape[1]):
        picked = jnp.concatenate([pick(lanes(q, 2 * g)), pick(lanes(q, 2 * g + 1))], axis=1)
        product = jnp.dot(picked, spread[q, g], preferred_element_type=F32)
        middle[q, pl.ds(first, rows), g * LANES : (g + 1) * LANES] = product.astype(BF16)


def apply_left(r, joined, starts, middle):
    factors, width = middle.shape[0], joined.shape[1]
    picked = [middle[q, aligned(starts(q, r), width), :] for q in range(factors)]
    return jnp.dot(joined[r], jnp.concatenate(picked, axis=0), preferred_element_type=F32)


class Plan:
    def __init__(self, factors, blocks, pieces, other):
        self.blocks = blocks
        self.other = other
        self.lanes = 0
        self.rows = factors * blocks
        self.uses = 2 * factors * blocks
        self.slot = 3 * factors * blocks
        self.whole = self.slot + blocks * blocks
        self.order = self.whole + pieces
        self.begin = self.order + blocks
        self.mirror = self.begin + pieces + 1
        self.size = self.mirror + 1


def make_plan(fixed, ends, plan, layout, columns, packing, slot, scalars):
    factors, blocks = columns.shape[0], columns.shape[2]

    def clear(i, carry):
        scalars[plan.uses + i] = 0
        return carry

    def offsets(s, carry):
        for q in range(factors):
            at = packing[layout.place + columns[q, 1, s]]
            scalars[plan.lanes + q * blocks + s] = columns[q, 0, s] // 2 * LANES
            scalars[plan.rows + q * blocks + s] = at * (LANES // 2)
            use = plan.uses + q * blocks + at
            scalars[use] = scalars[use] + 1
        return carry

    def locate(i, carry):
        for n in range(2):
            at = packing[layout.slot + 2 * i + n]
            scalars[plan.slot + 2 * i + n] = (at + n) % 2 * plan.other + at // 2 * LANES
        return carry

    lax.fori_loop(0, factors * blocks, clear, 0)
    lax.fori_loop(0, blocks, offsets, 0)
    lax.fori_loop(fixed * blocks // 2, blocks * blocks // 2, locate, 0)
    found, low = jnp.int32(0), jnp.int32(0)
    for j, end in enumerate(ends):

        def ready(at, n, end=end):
            return n + (jnp.minimum(packing[layout.used + at + 1], ends[-1]) <= end).astype(jnp.int32)

        high = lax.fori_loop(fixed, blocks, ready, jnp.int32(fixed)) if j else jnp.int32(fixed)
        scalars[plan.whole + j] = high
        scalars[plan.begin + j] = found

        def one(r, found, low=low, high=high):
            last = packing[layout.place + columns[0, 1, r]]
            for q in range(1, factors):
                last = jnp.maximum(last, packing[layout.place + columns[q, 1, r]])
            here = jnp.logical_and(last >= low, last < high)

            @pl.when(here)
            def _():
                scalars[plan.order + found] = r

            return found + here.astype(jnp.int32)

        found, low = lax.fori_loop(0, blocks, one, found), high
    scalars[plan.begin + len(ends)] = found
    scalars[plan.mirror] = slot[0]


def own_kernel(
    fixed,
    ends,
    plan,
    layout,
    columns,
    packing,
    slot,
    d_all,
    b_all,
    source,
    dressed,
    spread_d,
    joined_b,
    scalars,
    spread_b,
    joined_d,
    middle,
):
    factors, blocks, width = d_all.shape[:3]
    size = source.shape[1]
    make_plan(fixed, ends, plan, layout, columns, packing, slot, scalars)
    spread_right(b_all, columns, 1, spread_b)
    join_left(d_all, joined_d)
    spread_right(d_all, columns, 0, spread_d)
    join_left(b_all, joined_b)
    step = min(256, size)

    def right(q, carry):
        for m in range(0, size, step):
            apply_right(
                lambda lane: source[0, m : m + step, aligned(lane, LANES)],
                lambda q, s: columns[q, 1, s] // 2 * LANES,
                spread_b,
                q,
                middle,
                m,
                step,
            )
        return carry

    def left(r, carry):
        block = apply_left(r, joined_d, lambda q, r: columns[q, 0, r] * width, middle)
        dressed[aligned(r * width, width), :] = block.astype(BF16)
        return carry

    lax.fori_loop(0, factors, right, 0)
    lax.fori_loop(0, blocks, left, 0)


def own_pair(fixed, ends, plan, layout, columns, packing, slot, d_all, b_all, amplitudes):
    factors, blocks, width = d_all.shape[:3]
    size = amplitudes.shape[1]
    spread = (factors, blocks // 2, 2 * LANES, LANES)
    joined = (blocks, width, factors * width)
    return pl.pallas_call(
        functools.partial(own_kernel, fixed, ends, plan, layout),
        in_specs=[SCALARS, SCALARS, SCALARS, WHOLE, WHOLE, WHOLE],
        out_specs=[WHOLE, WHOLE, WHOLE, SCALARS],
        out_shape=[
            pltpu.VMEM((size, size), BF16),
            pltpu.VMEM(spread, BF16),
            pltpu.VMEM(joined, BF16),
            pltpu.SMEM((plan.size,), jnp.int32),
        ],
        scratch_shapes=[
            pltpu.VMEM(spread, BF16),
            pltpu.VMEM(joined, BF16),
            pltpu.VMEM((factors, size, size), BF16),
        ],
        compiler_params=params(),
        name="own",
    )(columns, packing, slot, d_all, b_all, amplitudes)


def finish_rows(begin, end, plan, scalars, joined_b, dressed, middle, out, ready, sems):
    blocks, width = joined_b.shape[:2]

    def leave(i):
        r = scalars[plan.order + i]
        return pltpu.make_async_copy(ready.at[r], out.at[aligned(r * width, width), :], sems.at[r])

    def left(i, carry):
        totals = []
        for n in range(2):
            r = scalars[plan.order + jnp.minimum(begin + 2 * i + n, end - 1)]
            mirrored = apply_left(r, joined_b, lambda q, r: scalars[plan.rows + q * blocks + r], middle)
            own = dressed[aligned(r * width, width), :].astype(F32)
            totals.append((own + mirrored.astype(BF16).astype(F32)).astype(BF16))
        for n, total in enumerate(totals):
            at = begin + 2 * i + n
            ready[jnp.where(at < end, scalars[plan.order + jnp.minimum(at, end - 1)], blocks)] = total

            @pl.when(at < end)
            def _(at=at):
                leave(at).start()

        return carry

    def wait(i, carry):
        leave(i).wait()
        return carry

    lax.fori_loop(0, (end - begin + 1) // 2, left, 0)
    lax.fori_loop(begin, end, wait, 0)


def opening_kernel(plan, scalars, piece, spread_d, joined_b, dressed, middle, packed, out, ready, sems):
    slot, blocks = scalars[plan.mirror], joined_b.shape[0]
    rows = piece.shape[1]
    packed[...] = jnp.zeros(packed.shape, BF16)
    for q in range(spread_d.shape[0]):
        apply_right(
            lambda lane: piece[slot, :, aligned(lane, LANES)],
            lambda q, s: scalars[plan.lanes + q * blocks + s],
            spread_d,
            q,
            middle,
            0,
            rows,
        )
    end = scalars[plan.begin + 1]
    finish_rows(0, end, plan, scalars, joined_b, dressed, middle, out, ready, sems)


def packed_kernel(j, last, starts, plan, scalars, spread_d, joined_b, dressed, *rest):
    pieces, rest = rest[: len(starts)], rest[len(starts) + 3 :]
    middle, packed, out, row, ready, sems = rest
    slot, factors = scalars[plan.mirror], spread_d.shape[0]
    blocks, width = joined_b.shape[:2]
    for start, piece in zip(starts, pieces):
        for lane in range(0, piece.shape[2], LANES):
            tile, at = piece[slot, :, lane : lane + LANES], start * width + lane
            packed[:, at : at + LANES] = tile
            packed[:, plan.other + at : plan.other + at + LANES] = swap_halves(tile)

    fixed = scalars[plan.whole]
    before, after = scalars[plan.whole + j - 1], scalars[plan.whole + j]
    left_half = lax.broadcasted_iota(jnp.int32, (width, LANES), 1) < width

    def take(i, carry):
        first = jnp.maximum(jnp.minimum(before + 2 * i, after - 2), fixed)
        for n in range(2):
            for k in range(0, blocks, 2):
                tiles = [packed[:, aligned(scalars[plan.slot + (first + n) * blocks + k + m], LANES)] for m in range(2)]
                row[n * width : (n + 1) * width, k * width : (k + 2) * width] = jnp.where(left_half, *tiles)
        for q in range(factors):
            uses = plan.uses + q * blocks + first
            skip = last and scalars[uses] + scalars[uses + 1] == 0

            def right(q=q):
                apply_right(
                    lambda lane: row[:, aligned(lane, LANES)],
                    lambda q, s: scalars[plan.lanes + q * blocks + s],
                    spread_d,
                    q,
                    middle,
                    pl.multiple_of(first * width, width),
                    2 * width,
                )

            if last:
                pl.when(jnp.logical_not(skip))(right)
            else:
                right()

        return carry

    lax.fori_loop(0, (after - before + 1) // 2, take, 0)
    begin, end = scalars[plan.begin + j], scalars[plan.begin + j + 1]
    finish_rows(begin, end, plan, scalars, joined_b, dressed, middle, out, ready, sems)


def mirror_piece(j, last, starts, slots, plan, scalars, pieces, spread_d, joined_b, dressed, state):
    size, (blocks, width) = dressed.shape[0], joined_b.shape[:2]
    shapes = [
        pltpu.VMEM((spread_d.shape[0], size, size), BF16),
        pltpu.VMEM((width, 2 * slots * width), BF16),
        jax.ShapeDtypeStruct((size, size), BF16),
    ]
    scratch = [pltpu.VMEM((blocks + 1, width, size), BF16), pltpu.SemaphoreType.DMA((blocks,))]
    if j == 0:
        kernel, given = functools.partial(opening_kernel, plan), (scalars, *pieces, spread_d, joined_b, dressed)
    else:
        kernel, given = functools.partial(packed_kernel, j, last, starts, plan), (scalars, spread_d, joined_b, dressed, *pieces)
        scratch = [pltpu.VMEM((2 * width, size), BF16)] + scratch
    return pl.pallas_call(
        kernel,
        in_specs=[SCALARS] + [WHOLE] * (len(given) - 1) + [WHOLE, WHOLE, FAR][: len(state)],
        out_specs=[WHOLE, WHOLE, FAR],
        out_shape=shapes,
        scratch_shapes=scratch,
        input_output_aliases={len(given) + i: i for i in range(len(state))},
        compiler_params=params(),
        name="mirror",
    )(*given, *state)


def cuts(blocks):
    fixed = blocks // 4
    slots = (blocks - fixed) * blocks
    return fixed, [slots * m // 192 // 2 * 2 for m in (0, 64, 128, 160, 180)], slots


def later(arrays, *after):
    return lax.optimization_barrier((arrays, after))[0]


def shards(amplitudes, mirror_slot, d_values, d_cols, b_values, b_cols):
    pairs = lax.axis_size("pair")
    perm = [(i, (i + pairs // 2) % pairs) for i in range(pairs)]
    assert amplitudes.shape[0] == 1
    blocks, width = d_values.shape[1], d_values.shape[2]

    fixed, marks, slots = cuts(blocks)
    ends = [0] + marks[1:]
    layout = Layout(blocks)
    plan = Plan(lax.axis_size("fac") * d_cols.shape[0], blocks, len(ends), slots * width)
    amplitudes = pltpu.with_memory_space_constraint(amplitudes, pltpu.HBM)

    def send(piece):
        return lax.ppermute(piece, "pair", perm)

    def gather(array):
        return lax.all_gather(array, "fac", axis=0, tiled=True)

    head = turn(amplitudes, [0, fixed * width])[0]
    pieces = [[send(head)]]
    rest = turn(later(amplitudes, head), [fixed * width, blocks * width])[0]
    columns = gather(later(jnp.stack([d_cols, b_cols], axis=1), rest))
    spans = list(zip(marks, marks[1:]))
    packing, picked, over = pack_pieces(columns, [spans[0], (marks[-1], slots)], fixed, layout, rest)
    over = lax.cond(packing[layout.used + blocks] > marks[-1], send, lambda piece: piece, over)
    picked = later(picked, over)
    pieces.append([send(picked), over])
    picked = [picked, *pack_pieces(later(packing, picked), spans[1:], fixed, layout, rest)]
    d_all = gather(later(d_values, picked))
    pieces.append([send(later(picked[1], d_all))])
    b_all = gather(later(b_values, d_all))
    pieces.append([send(later(picked[2], b_all))])
    own = own_pair(fixed, ends, plan, layout, columns, packing, mirror_slot, d_all, b_all, amplitudes)
    dressed, spread_d, joined_b, scalars = own
    pieces.append([send(later(picked[3], dressed))])

    state = ()
    for j, arrived in enumerate(pieces):
        starts = [] if j == 0 else [marks[j - 1], marks[-1]][: len(arrived)]
        state = mirror_piece(j, j == len(pieces) - 1, starts, slots, plan, scalars, arrived, spread_d, joined_b, dressed, state)
    return state[2][None]


def solution(mesh):
    placed = (
        P(("pair", "fac"), None, None),
        P(("pair", "fac")),
        P("fac", None, None, None),
        P("fac", None),
        P("fac", None, None, None),
        P("fac", None),
    )
    return jax.shard_map(
        shards,
        mesh=mesh,
        in_specs=placed,
        out_specs=P(("pair", "fac"), None, None),
        check_vma=False,
    )
```

```python
import functools

import jax
import jax.numpy as jnp
from jax import lax
from jax.experimental import pallas as pl
from jax.experimental.pallas import tpu as pltpu
from jax.sharding import PartitionSpec as P

LANES = 128
BF16, F32 = jnp.bfloat16, jnp.float32
WHOLE = pl.BlockSpec(memory_space=pltpu.VMEM)
SCALARS = pl.BlockSpec(memory_space=pltpu.SMEM)
FAR = pl.BlockSpec(memory_space=pltpu.HBM)
VMEM_BYTES = 28 << 20


def params():
    return pltpu.CompilerParams(vmem_limit_bytes=VMEM_BYTES)


def aligned(start, size):
    return pl.ds(pl.multiple_of(start, size), size)


def strips_of(marks):
    return range(marks[0] // LANES * LANES, marks[-1], LANES)


def turn_kernel(marks, source, *rest):
    turned, strips, sems = rest[:-2], rest[-2], rest[-1]
    starts = strips_of(marks)
    copies = [
        pltpu.make_async_copy(source.at[0, :, lo : lo + LANES], strips.at[i], sems.at[i]) for i, lo in enumerate(starts)
    ]
    for copy in copies:
        copy.start()
    for i, lo in enumerate(starts):
        copies[i].wait()
        strip = strips[i].T
        for first, last, piece in zip(marks, marks[1:], turned):
            a, b = max(lo, first), min(lo + LANES, last)
            if a < b:
                piece[0, a - first : b - first, :] = strip[a - lo : b - lo, :]


def turn(amplitudes, marks):
    size = amplitudes.shape[1]
    count = len(strips_of(marks))
    return pl.pallas_call(
        functools.partial(turn_kernel, marks),
        in_specs=[FAR],
        out_specs=[WHOLE] * (len(marks) - 1),
        out_shape=[jax.ShapeDtypeStruct((1, b - a, size), BF16) for a, b in zip(marks, marks[1:])],
        scratch_shapes=[pltpu.VMEM((count, size, LANES), BF16), pltpu.SemaphoreType.DMA((count,))],
        compiler_params=params(),
        name="turn",
    )(amplitudes)


class Layout:
    def __init__(self, blocks):
        self.blocks = blocks
        self.place = 0
        self.used = blocks
        self.slot = 2 * blocks + 1
        self.block = self.slot + blocks * blocks
        self.size = self.block + blocks * blocks


def swap_halves(tile):
    half = tile.shape[1] // 2
    return jnp.concatenate([tile[:, half:], tile[:, :half]], axis=1)


def join_halves(low, low_swapped, high, high_swapped):
    low = jnp.where(low_swapped, swap_halves(low), low)
    high = jnp.where(high_swapped, swap_halves(high), high)
    lane = lax.broadcasted_iota(jnp.int32, low.shape, 1)
    return jnp.where(lane < low.shape[1] // 2, low, high)


def pack(start, piece, fixed, layout, scalars, turned):
    blocks = layout.blocks
    width = turned.shape[1] // (blocks - fixed)
    tiles = piece.shape[2] // LANES
    group = 4 if tiles % 4 == 0 else 2 if tiles % 2 == 0 else 1

    def half(slot):
        at = scalars[layout.block + slot]
        row, k = at // blocks, at % blocks
        return turned[0, aligned(row * width, width), aligned(k // 2 * LANES, LANES)], k % 2

    def fill(i, carry):
        for n in range(group):
            tile = i * group + n
            low, k_low = half(start + 2 * tile)
            high, k_high = half(start + 2 * tile + 1)
            piece[0, :, aligned(tile * LANES, LANES)] = join_halves(low, k_low == 1, high, k_high == 0)
        return carry

    lax.fori_loop(0, tiles // group, fill, 0)


def pack_kernel(starts, fixed, layout, scalars, turned, *pieces):
    for start, piece in zip(starts, pieces):
        pack(start, piece, fixed, layout, scalars, turned)


def pick_kernel(starts, fixed, layout, columns, turned, scalars, *rest):
    pieces, tally = rest[:-1], rest[-1]
    factors, blocks = columns.shape[0], columns.shape[2]

    def clear(c, carry):
        tally[c] = 0
        scalars[layout.place + c] = c
        scalars[layout.used + c] = 0
        for k in range(blocks):
            scalars[layout.block + c * blocks + k] = 0
        return carry

    def count(r, masks):
        left, right = [], []
        for q in range(factors):
            c = columns[q, 1, r]
            tally[c] = tally[c] + 1
            left.append(masks[0][q] | jnp.left_shift(1, c))
            right.append(masks[1][q] | jnp.left_shift(1, columns[q, 0, r]))
        return left, right

    lax.fori_loop(0, blocks, clear, 0)
    none = [jnp.int32(0)] * factors
    left, right = lax.fori_loop(0, blocks, count, (none, none))

    def select(at, used):
        def better(c, best):
            wins = tally[c] > best[0]
            return jnp.where(wins, tally[c], best[0]), jnp.where(wins, c, best[1])

        c = lax.fori_loop(fixed, blocks, better, (jnp.int32(-1), jnp.int32(fixed)))[1]
        tally[c] = -2
        scalars[layout.place + c] = at
        scalars[layout.used + at] = used
        read = jnp.int32(0)
        for q in range(factors):
            read = read | jnp.where(jnp.right_shift(left[q], c) & 1 == 1, right[q], 0)
        for k in range(blocks):
            bit = jnp.right_shift(read, k) & 1
            scalars[layout.block + used] = (c - fixed) * blocks + k
            scalars[layout.slot + at * blocks + k] = jnp.where(bit == 1, used, 0)
            used = used + bit
        return used

    scalars[layout.used + blocks] = lax.fori_loop(fixed, blocks, select, jnp.int32(0))

    pack_kernel(starts, fixed, layout, scalars, turned, *pieces)


def pack_pieces(given, spans, fixed, layout, turned):
    opening = given.ndim == 3
    blocks = layout.blocks
    width = turned.shape[1] // (blocks - fixed)
    shapes = [jax.ShapeDtypeStruct((1, width, (hi - lo) * width), BF16) for lo, hi in spans]
    kernel = functools.partial(pick_kernel if opening else pack_kernel, [lo for lo, _ in spans], fixed, layout)
    return pl.pallas_call(
        kernel,
        in_specs=[SCALARS, WHOLE],
        out_specs=[SCALARS] * opening + [WHOLE] * len(spans),
        out_shape=[jax.ShapeDtypeStruct((layout.size,), jnp.int32)] * opening + shapes,
        scratch_shapes=[pltpu.SMEM((blocks,), jnp.int32)] * opening,
        compiler_params=params(),
        name="pack",
    )(given, turned)


def spread_right(values, columns, side, spread):
    factors, blocks, width = values.shape[:3]
    spread[...] = jnp.zeros(spread.shape, BF16)

    def one(group, carry):
        for q in range(factors):
            for i in range(2):
                s = 2 * group + i
                row = i * LANES + (columns[q, side, s] % 2) * width
                spread[q, group, aligned(row, width), i * width : (i + 1) * width] = values[q, s].T
        return carry

    lax.fori_loop(0, blocks // 2, one, 0)


def join_left(values, joined):
    factors, blocks, width = values.shape[:3]

    def one(r, carry):
        for q in range(factors):
            joined[r, :, q * width : (q + 1) * width] = values[q, r]
        return carry

    lax.fori_loop(0, blocks, one, 0)


def apply_right(pick, lanes, spread, q, middle, first, rows):
    for g in range(spread.shape[1]):
        picked = jnp.concatenate([pick(lanes(q, 2 * g)), pick(lanes(q, 2 * g + 1))], axis=1)
        product = jnp.dot(picked, spread[q, g], preferred_element_type=F32)
        middle[q, pl.ds(first, rows), g * LANES : (g + 1) * LANES] = product.astype(BF16)


def apply_left(r, joined, starts, middle):
    factors, width = middle.shape[0], joined.shape[1]
    picked = [middle[q, aligned(starts(q, r), width), :] for q in range(factors)]
    return jnp.dot(joined[r], jnp.concatenate(picked, axis=0), preferred_element_type=F32)


class Plan:
    def __init__(self, factors, blocks, pieces, other):
        self.blocks = blocks
        self.other = other
        self.lanes = 0
        self.rows = factors * blocks
        self.uses = 2 * factors * blocks
        self.slot = 3 * factors * blocks
        self.whole = self.slot + blocks * blocks
        self.order = self.whole + pieces
        self.begin = self.order + blocks
        self.mirror = self.begin + pieces + 1
        self.size = self.mirror + 1


def make_plan(fixed, ends, plan, layout, columns, packing, slot, scalars):
    factors, blocks = columns.shape[0], columns.shape[2]

    def clear(i, carry):
        scalars[plan.uses + i] = 0
        return carry

    def offsets(s, carry):
        for q in range(factors):
            at = packing[layout.place + columns[q, 1, s]]
            scalars[plan.lanes + q * blocks + s] = columns[q, 0, s] // 2 * LANES
            scalars[plan.rows + q * blocks + s] = at * (LANES // 2)
            use = plan.uses + q * blocks + at
            scalars[use] = scalars[use] + 1
        return carry

    def locate(i, carry):
        for n in range(2):
            at = packing[layout.slot + 2 * i + n]
            scalars[plan.slot + 2 * i + n] = (at + n) % 2 * plan.other + at // 2 * LANES
        return carry

    lax.fori_loop(0, factors * blocks, clear, 0)
    lax.fori_loop(0, blocks, offsets, 0)
    lax.fori_loop(fixed * blocks // 2, blocks * blocks // 2, locate, 0)
    found, low = jnp.int32(0), jnp.int32(0)
    for j, end in enumerate(ends):

        def ready(at, n, end=end):
            return n + (jnp.minimum(packing[layout.used + at + 1], ends[-1]) <= end).astype(jnp.int32)

        high = lax.fori_loop(fixed, blocks, ready, jnp.int32(fixed)) if j else jnp.int32(fixed)
        scalars[plan.whole + j] = high
        scalars[plan.begin + j] = found

        def one(r, found, low=low, high=high):
            last = packing[layout.place + columns[0, 1, r]]
            for q in range(1, factors):
                last = jnp.maximum(last, packing[layout.place + columns[q, 1, r]])
            here = jnp.logical_and(last >= low, last < high)

            @pl.when(here)
            def _():
                scalars[plan.order + found] = r

            return found + here.astype(jnp.int32)

        found, low = lax.fori_loop(0, blocks, one, found), high
    scalars[plan.begin + len(ends)] = found
    scalars[plan.mirror] = slot[0]


def own_kernel(
    fixed,
    ends,
    plan,
    layout,
    columns,
    packing,
    slot,
    d_all,
    b_all,
    source,
    dressed,
    spread_d,
    joined_b,
    scalars,
    spread_b,
    joined_d,
    middle,
):
    factors, blocks, width = d_all.shape[:3]
    size = source.shape[1]
    make_plan(fixed, ends, plan, layout, columns, packing, slot, scalars)
    spread_right(b_all, columns, 1, spread_b)
    join_left(d_all, joined_d)
    spread_right(d_all, columns, 0, spread_d)
    join_left(b_all, joined_b)
    step = min(256, size)

    def right(q, carry):
        for m in range(0, size, step):
            apply_right(
                lambda lane: source[0, m : m + step, aligned(lane, LANES)],
                lambda q, s: columns[q, 1, s] // 2 * LANES,
                spread_b,
                q,
                middle,
                m,
                step,
            )
        return carry

    def left(r, carry):
        block = apply_left(r, joined_d, lambda q, r: columns[q, 0, r] * width, middle)
        dressed[aligned(r * width, width), :] = block.astype(BF16)
        return carry

    lax.fori_loop(0, factors, right, 0)
    lax.fori_loop(0, blocks, left, 0)


def own_pair(fixed, ends, plan, layout, columns, packing, slot, d_all, b_all, amplitudes):
    factors, blocks, width = d_all.shape[:3]
    size = amplitudes.shape[1]
    spread = (factors, blocks // 2, 2 * LANES, LANES)
    joined = (blocks, width, factors * width)
    return pl.pallas_call(
        functools.partial(own_kernel, fixed, ends, plan, layout),
        in_specs=[SCALARS, SCALARS, SCALARS, WHOLE, WHOLE, WHOLE],
        out_specs=[WHOLE, WHOLE, WHOLE, SCALARS],
        out_shape=[
            pltpu.VMEM((size, size), BF16),
            pltpu.VMEM(spread, BF16),
            pltpu.VMEM(joined, BF16),
            pltpu.SMEM((plan.size,), jnp.int32),
        ],
        scratch_shapes=[
            pltpu.VMEM(spread, BF16),
            pltpu.VMEM(joined, BF16),
            pltpu.VMEM((factors, size, size), BF16),
        ],
        compiler_params=params(),
        name="own",
    )(columns, packing, slot, d_all, b_all, amplitudes)


def finish_rows(begin, end, plan, scalars, joined_b, dressed, middle, out, ready, sems):
    blocks, width = joined_b.shape[:2]

    def leave(i):
        r = scalars[plan.order + i]
        return pltpu.make_async_copy(ready.at[r], out.at[aligned(r * width, width), :], sems.at[r])

    def left(i, carry):
        totals = []
        for n in range(2):
            r = scalars[plan.order + jnp.minimum(begin + 2 * i + n, end - 1)]
            mirrored = apply_left(r, joined_b, lambda q, r: scalars[plan.rows + q * blocks + r], middle)
            own = dressed[aligned(r * width, width), :].astype(F32)
            totals.append((own + mirrored.astype(BF16).astype(F32)).astype(BF16))
        for n, total in enumerate(totals):
            at = begin + 2 * i + n
            ready[jnp.where(at < end, scalars[plan.order + jnp.minimum(at, end - 1)], blocks)] = total

            @pl.when(at < end)
            def _(at=at):
                leave(at).start()

        return carry

    def wait(i, carry):
        leave(i).wait()
        return carry

    lax.fori_loop(0, (end - begin + 1) // 2, left, 0)
    lax.fori_loop(begin, end, wait, 0)


def opening_kernel(plan, scalars, piece, spread_d, joined_b, dressed, middle, packed, out, token, ready, sems):
    slot, blocks = scalars[plan.mirror], joined_b.shape[0]
    rows = piece.shape[1]
    packed[...] = jnp.zeros(packed.shape, BF16)
    token[...] = jnp.zeros(token.shape, F32)
    for q in range(spread_d.shape[0]):
        apply_right(
            lambda lane: piece[slot, :, aligned(lane, LANES)],
            lambda q, s: scalars[plan.lanes + q * blocks + s],
            spread_d,
            q,
            middle,
            0,
            rows,
        )
    end = scalars[plan.begin + 1]
    finish_rows(0, end, plan, scalars, joined_b, dressed, middle, out, ready, sems)


def packed_kernel(j, last, starts, plan, scalars, spread_d, joined_b, dressed, *rest):
    pieces, rest = rest[: len(starts)], rest[len(starts) + 3 :]
    middle, packed, out, row, ready, sems = rest
    slot, factors = scalars[plan.mirror], spread_d.shape[0]
    blocks, width = joined_b.shape[:2]
    for start, piece in zip(starts, pieces):
        for lane in range(0, piece.shape[2], LANES):
            tile, at = piece[slot, :, lane : lane + LANES], start * width + lane
            packed[:, at : at + LANES] = tile
            packed[:, plan.other + at : plan.other + at + LANES] = swap_halves(tile)

    fixed = scalars[plan.whole]
    before, after = scalars[plan.whole + j - 1], scalars[plan.whole + j]
    left_half = lax.broadcasted_iota(jnp.int32, (width, LANES), 1) < width

    def take(i, carry):
        first = jnp.maximum(jnp.minimum(before + 2 * i, after - 2), fixed)
        for n in range(2):
            for k in range(0, blocks, 2):
                tiles = [packed[:, aligned(scalars[plan.slot + (first + n) * blocks + k + m], LANES)] for m in range(2)]
                row[n * width : (n + 1) * width, k * width : (k + 2) * width] = jnp.where(left_half, *tiles)
        for q in range(factors):
            uses = plan.uses + q * blocks + first
            skip = last and scalars[uses] + scalars[uses + 1] == 0

            def right(q=q):
                apply_right(
                    lambda lane: row[:, aligned(lane, LANES)],
                    lambda q, s: scalars[plan.lanes + q * blocks + s],
                    spread_d,
                    q,
                    middle,
                    pl.multiple_of(first * width, width),
                    2 * width,
                )

            if last:
                pl.when(jnp.logical_not(skip))(right)
            else:
                right()

        return carry

    lax.fori_loop(0, (after - before + 1) // 2, take, 0)
    begin, end = scalars[plan.begin + j], scalars[plan.begin + j + 1]
    finish_rows(begin, end, plan, scalars, joined_b, dressed, middle, out, ready, sems)


def mirror_piece(j, last, starts, slots, plan, scalars, pieces, spread_d, joined_b, dressed, state):
    size, (blocks, width) = dressed.shape[0], joined_b.shape[:2]
    shapes = [
        pltpu.VMEM((spread_d.shape[0], size, size), BF16),
        pltpu.VMEM((width, 2 * slots * width), BF16),
        jax.ShapeDtypeStruct((size, size), BF16),
    ]
    scratch = [pltpu.VMEM((blocks + 1, width, size), BF16), pltpu.SemaphoreType.DMA((blocks,))]
    if j == 0:
        shapes.append(jax.ShapeDtypeStruct((8, LANES), F32))
        kernel, given = functools.partial(opening_kernel, plan), (scalars, *pieces, spread_d, joined_b, dressed)
    else:
        kernel, given = functools.partial(packed_kernel, j, last, starts, plan), (scalars, spread_d, joined_b, dressed, *pieces)
        scratch = [pltpu.VMEM((2 * width, size), BF16)] + scratch
    return pl.pallas_call(
        kernel,
        in_specs=[SCALARS] + [WHOLE] * (len(given) - 1) + [WHOLE, WHOLE, FAR][: len(state)],
        out_specs=[WHOLE, WHOLE, FAR, WHOLE][: len(shapes)],
        out_shape=shapes,
        scratch_shapes=scratch,
        input_output_aliases={len(given) + i: i for i in range(len(state))},
        compiler_params=params(),
        name="mirror",
    )(*given, *state)


def cuts(blocks):
    fixed = 3 * blocks // 16
    slots = (blocks - fixed) * blocks
    return fixed, [slots * m // 208 // 2 * 2 for m in (0, 48, 96, 144, 172, 192)], slots


def later(arrays, *after):
    return lax.optimization_barrier((arrays, after))[0]


def shards(amplitudes, mirror_slot, d_values, d_cols, b_values, b_cols):
    pairs = lax.axis_size("pair")
    perm = [(i, (i + pairs // 2) % pairs) for i in range(pairs)]
    assert amplitudes.shape[0] == 1
    blocks, width = d_values.shape[1], d_values.shape[2]

    fixed, marks, slots = cuts(blocks)
    ends = [0] + marks[1:]
    layout = Layout(blocks)
    plan = Plan(lax.axis_size("fac") * d_cols.shape[0], blocks, len(ends), slots * width)
    amplitudes = pltpu.with_memory_space_constraint(amplitudes, pltpu.HBM)

    def send(piece):
        return lax.ppermute(piece, "pair", perm)

    def gather(array):
        return lax.all_gather(array, "fac", axis=0, tiled=True)

    head = turn(amplitudes, [0, fixed * width])[0]
    pieces = [[send(head)]]
    rest = turn(later(amplitudes, head), [fixed * width, blocks * width])[0]
    columns = gather(later(jnp.stack([d_cols, b_cols], axis=1), rest))
    spans = list(zip(marks, marks[1:]))
    packing, picked, over = pack_pieces(columns, [spans[0], (marks[-1], slots)], fixed, layout, rest)
    over = lax.cond(packing[layout.used + blocks] > marks[-1], send, lambda piece: piece, over)
    picked = later(picked, over)
    pieces.append([send(picked), over])
    picked = [picked, *pack_pieces(later(packing, picked), spans[1:], fixed, layout, rest)]
    d_all = gather(later(d_values, picked))
    pieces.append([send(later(picked[1], d_all))])
    b_all = gather(later(b_values, d_all))
    pieces.append([send(later(picked[2], b_all))])
    own = own_pair(fixed, ends, plan, layout, columns, packing, mirror_slot, d_all, b_all, amplitudes)
    dressed, spread_d, joined_b, scalars = own
    pieces.append([send(later(picked[3], dressed))])

    state = ()
    for j in range(len(ends)):
        if j == 1:
            *state, token = state
            pieces.append([send(later(picked[4], token))])
        arrived = pieces[j]
        starts = [] if j == 0 else [marks[j - 1], marks[-1]][: len(arrived)]
        state = mirror_piece(j, j == len(ends) - 1, starts, slots, plan, scalars, arrived, spread_d, joined_b, dressed, state)
    return state[2][None]


def solution(mesh):
    placed = (
        P(("pair", "fac"), None, None),
        P(("pair", "fac")),
        P("fac", None, None, None),
        P("fac", None),
        P("fac", None, None, None),
        P("fac", None),
    )
    return jax.shard_map(
        shards,
        mesh=mesh,
        in_specs=placed,
        out_specs=P(("pair", "fac"), None, None),
        check_vma=False,
    )
```

```python
import functools

import jax
import jax.numpy as jnp
from jax import lax
from jax.experimental import pallas as pl
from jax.experimental.pallas import tpu as pltpu
from jax.sharding import PartitionSpec as P

LANES = 128
BF16, F32 = jnp.bfloat16, jnp.float32
WHOLE = pl.BlockSpec(memory_space=pltpu.VMEM)
SCALARS = pl.BlockSpec(memory_space=pltpu.SMEM)
FAR = pl.BlockSpec(memory_space=pltpu.HBM)
VMEM_BYTES = 28 << 20


def params():
    return pltpu.CompilerParams(vmem_limit_bytes=VMEM_BYTES)


def aligned(start, size):
    return pl.ds(pl.multiple_of(start, size), size)


def strips_of(marks):
    return range(marks[0] // LANES * LANES, marks[-1], LANES)


def turn_kernel(marks, source, *rest):
    turned, strips, sems = rest[:-2], rest[-2], rest[-1]
    starts = strips_of(marks)
    copies = [
        pltpu.make_async_copy(source.at[0, :, lo : lo + LANES], strips.at[i], sems.at[i]) for i, lo in enumerate(starts)
    ]
    for copy in copies:
        copy.start()
    for i, lo in enumerate(starts):
        copies[i].wait()
        strip = strips[i].T
        for first, last, piece in zip(marks, marks[1:], turned):
            a, b = max(lo, first), min(lo + LANES, last)
            if a < b:
                piece[0, a - first : b - first, :] = strip[a - lo : b - lo, :]


def turn(amplitudes, marks):
    size = amplitudes.shape[1]
    count = len(strips_of(marks))
    return pl.pallas_call(
        functools.partial(turn_kernel, marks),
        in_specs=[FAR],
        out_specs=[WHOLE] * (len(marks) - 1),
        out_shape=[jax.ShapeDtypeStruct((1, b - a, size), BF16) for a, b in zip(marks, marks[1:])],
        scratch_shapes=[pltpu.VMEM((count, size, LANES), BF16), pltpu.SemaphoreType.DMA((count,))],
        compiler_params=params(),
        name="turn",
    )(amplitudes)


class Layout:
    def __init__(self, blocks):
        self.blocks = blocks
        self.place = 0
        self.used = blocks
        self.slot = 2 * blocks + 1
        self.block = self.slot + blocks * blocks
        self.size = self.block + blocks * blocks


def swap_halves(tile):
    half = tile.shape[1] // 2
    return jnp.concatenate([tile[:, half:], tile[:, :half]], axis=1)


def join_halves(low, low_swapped, high, high_swapped):
    low = jnp.where(low_swapped, swap_halves(low), low)
    high = jnp.where(high_swapped, swap_halves(high), high)
    lane = lax.broadcasted_iota(jnp.int32, low.shape, 1)
    return jnp.where(lane < low.shape[1] // 2, low, high)


def pack(start, piece, fixed, layout, scalars, turned):
    blocks = layout.blocks
    width = turned.shape[1] // (blocks - fixed)
    tiles = piece.shape[2] // LANES
    group = 4 if tiles % 4 == 0 else 2 if tiles % 2 == 0 else 1

    def half(slot):
        at = scalars[layout.block + slot]
        row, k = at // blocks, at % blocks
        return turned[0, aligned(row * width, width), aligned(k // 2 * LANES, LANES)], k % 2

    def fill(i, carry):
        for n in range(group):
            tile = i * group + n
            low, k_low = half(start + 2 * tile)
            high, k_high = half(start + 2 * tile + 1)
            piece[0, :, aligned(tile * LANES, LANES)] = join_halves(low, k_low == 1, high, k_high == 0)
        return carry

    lax.fori_loop(0, tiles // group, fill, 0)


def pack_kernel(starts, fixed, layout, scalars, turned, *pieces):
    for start, piece in zip(starts, pieces):
        pack(start, piece, fixed, layout, scalars, turned)


def pick_kernel(starts, fixed, layout, columns, turned, scalars, *rest):
    pieces, tally = rest[:-1], rest[-1]
    factors, blocks = columns.shape[0], columns.shape[2]

    def clear(c, carry):
        tally[c] = 0
        scalars[layout.place + c] = c
        scalars[layout.used + c] = 0
        for k in range(blocks):
            scalars[layout.block + c * blocks + k] = 0
        return carry

    def count(r, masks):
        left, right = [], []
        for q in range(factors):
            c = columns[q, 1, r]
            tally[c] = tally[c] + 1
            left.append(masks[0][q] | jnp.left_shift(1, c))
            right.append(masks[1][q] | jnp.left_shift(1, columns[q, 0, r]))
        return left, right

    lax.fori_loop(0, blocks, clear, 0)
    none = [jnp.int32(0)] * factors
    left, right = lax.fori_loop(0, blocks, count, (none, none))

    def select(at, used):
        most, c = tally[fixed], jnp.int32(fixed)
        for other in range(fixed + 1, blocks):
            n = tally[other]
            most, c = jnp.maximum(most, n), jnp.where(n > most, other, c)
        tally[c] = -2
        scalars[layout.place + c] = at
        scalars[layout.used + at] = used
        read = jnp.int32(0)
        for q in range(factors):
            read = read | jnp.where(jnp.right_shift(left[q], c) & 1 == 1, right[q], 0)
        for k in range(blocks):
            bit = jnp.right_shift(read, k) & 1
            scalars[layout.block + used] = (c - fixed) * blocks + k
            scalars[layout.slot + at * blocks + k] = jnp.where(bit == 1, used, 0)
            used = used + bit
        return used

    scalars[layout.used + blocks] = lax.fori_loop(fixed, blocks, select, jnp.int32(0))

    pack_kernel(starts, fixed, layout, scalars, turned, *pieces)


def pack_pieces(given, spans, fixed, layout, turned):
    opening = given.ndim == 3
    blocks = layout.blocks
    width = turned.shape[1] // (blocks - fixed)
    shapes = [jax.ShapeDtypeStruct((1, width, (hi - lo) * width), BF16) for lo, hi in spans]
    kernel = functools.partial(pick_kernel if opening else pack_kernel, [lo for lo, _ in spans], fixed, layout)
    return pl.pallas_call(
        kernel,
        in_specs=[SCALARS, WHOLE],
        out_specs=[SCALARS] * opening + [WHOLE] * len(spans),
        out_shape=[jax.ShapeDtypeStruct((layout.size,), jnp.int32)] * opening + shapes,
        scratch_shapes=[pltpu.SMEM((blocks,), jnp.int32)] * opening,
        compiler_params=params(),
        name="pack",
    )(given, turned)


def spread_right(values, columns, side, spread):
    factors, blocks, width = values.shape[:3]
    spread[...] = jnp.zeros(spread.shape, BF16)

    def one(group, carry):
        for q in range(factors):
            for i in range(2):
                s = 2 * group + i
                row = i * LANES + (columns[q, side, s] % 2) * width
                spread[q, group, aligned(row, width), i * width : (i + 1) * width] = values[q, s].T
        return carry

    lax.fori_loop(0, blocks // 2, one, 0)


def join_left(values, joined):
    factors, blocks, width = values.shape[:3]

    def one(r, carry):
        for q in range(factors):
            joined[r, :, q * width : (q + 1) * width] = values[q, r]
        return carry

    lax.fori_loop(0, blocks, one, 0)


def apply_right(pick, lanes, spread, q, middle, first, rows):
    for g in range(spread.shape[1]):
        picked = jnp.concatenate([pick(lanes(q, 2 * g)), pick(lanes(q, 2 * g + 1))], axis=1)
        product = jnp.dot(picked, spread[q, g], preferred_element_type=F32)
        middle[q, pl.ds(first, rows), g * LANES : (g + 1) * LANES] = product.astype(BF16)


def apply_left(r, joined, starts, middle):
    factors, width = middle.shape[0], joined.shape[1]
    picked = [middle[q, aligned(starts(q, r), width), :] for q in range(factors)]
    return jnp.dot(joined[r], jnp.concatenate(picked, axis=0), preferred_element_type=F32)


class Plan:
    def __init__(self, factors, blocks, pieces, other):
        self.blocks = blocks
        self.other = other
        self.lanes = 0
        self.rows = factors * blocks
        self.uses = 2 * factors * blocks
        self.slot = 3 * factors * blocks
        self.whole = self.slot + blocks * blocks
        self.order = self.whole + pieces
        self.begin = self.order + blocks
        self.mirror = self.begin + pieces + 1
        self.size = self.mirror + 1


def make_plan(fixed, ends, plan, layout, columns, packing, slot, scalars):
    factors, blocks = columns.shape[0], columns.shape[2]

    def clear(i, carry):
        scalars[plan.uses + i] = 0
        return carry

    def offsets(s, carry):
        for q in range(factors):
            at = packing[layout.place + columns[q, 1, s]]
            scalars[plan.lanes + q * blocks + s] = columns[q, 0, s] // 2 * LANES
            scalars[plan.rows + q * blocks + s] = at * (LANES // 2)
            use = plan.uses + q * blocks + at
            scalars[use] = scalars[use] + 1
        return carry

    def locate(i, carry):
        for n in range(2):
            at = packing[layout.slot + 2 * i + n]
            scalars[plan.slot + 2 * i + n] = (at + n) % 2 * plan.other + at // 2 * LANES
        return carry

    lax.fori_loop(0, factors * blocks, clear, 0)
    lax.fori_loop(0, blocks, offsets, 0)
    lax.fori_loop(fixed * blocks // 2, blocks * blocks // 2, locate, 0)
    found, low = jnp.int32(0), jnp.int32(0)
    for j, end in enumerate(ends):

        def ready(at, n, end=end):
            return n + (jnp.minimum(packing[layout.used + at + 1], ends[-1]) <= end).astype(jnp.int32)

        high = lax.fori_loop(fixed, blocks, ready, jnp.int32(fixed)) if j else jnp.int32(fixed)
        scalars[plan.whole + j] = high
        scalars[plan.begin + j] = found

        def one(r, found, low=low, high=high):
            last = packing[layout.place + columns[0, 1, r]]
            for q in range(1, factors):
                last = jnp.maximum(last, packing[layout.place + columns[q, 1, r]])
            here = jnp.logical_and(last >= low, last < high)

            @pl.when(here)
            def _():
                scalars[plan.order + found] = r

            return found + here.astype(jnp.int32)

        found, low = lax.fori_loop(0, blocks, one, found), high
    scalars[plan.begin + len(ends)] = found
    scalars[plan.mirror] = slot[0]


def own_kernel(
    fixed,
    ends,
    plan,
    layout,
    columns,
    packing,
    slot,
    d_all,
    b_all,
    source,
    dressed,
    spread_d,
    joined_b,
    scalars,
    spread_b,
    joined_d,
    middle,
):
    factors, blocks, width = d_all.shape[:3]
    size = source.shape[1]
    make_plan(fixed, ends, plan, layout, columns, packing, slot, scalars)
    spread_right(b_all, columns, 1, spread_b)
    join_left(d_all, joined_d)
    spread_right(d_all, columns, 0, spread_d)
    join_left(b_all, joined_b)
    step = min(256, size)

    def right(q, carry):
        for m in range(0, size, step):
            apply_right(
                lambda lane: source[0, m : m + step, aligned(lane, LANES)],
                lambda q, s: columns[q, 1, s] // 2 * LANES,
                spread_b,
                q,
                middle,
                m,
                step,
            )
        return carry

    def left(r, carry):
        block = apply_left(r, joined_d, lambda q, r: columns[q, 0, r] * width, middle)
        dressed[aligned(r * width, width), :] = block.astype(BF16)
        return carry

    lax.fori_loop(0, factors, right, 0)
    lax.fori_loop(0, blocks, left, 0)


def own_pair(fixed, ends, plan, layout, columns, packing, slot, d_all, b_all, amplitudes):
    factors, blocks, width = d_all.shape[:3]
    size = amplitudes.shape[1]
    spread = (factors, blocks // 2, 2 * LANES, LANES)
    joined = (blocks, width, factors * width)
    return pl.pallas_call(
        functools.partial(own_kernel, fixed, ends, plan, layout),
        in_specs=[SCALARS, SCALARS, SCALARS, WHOLE, WHOLE, WHOLE],
        out_specs=[WHOLE, WHOLE, WHOLE, SCALARS],
        out_shape=[
            pltpu.VMEM((size, size), BF16),
            pltpu.VMEM(spread, BF16),
            pltpu.VMEM(joined, BF16),
            pltpu.SMEM((plan.size,), jnp.int32),
        ],
        scratch_shapes=[
            pltpu.VMEM(spread, BF16),
            pltpu.VMEM(joined, BF16),
            pltpu.VMEM((factors, size, size), BF16),
        ],
        compiler_params=params(),
        name="own",
    )(columns, packing, slot, d_all, b_all, amplitudes)


def finish_rows(begin, end, plan, scalars, joined_b, dressed, middle, out, ready, sems):
    blocks, width = joined_b.shape[:2]

    def leave(i):
        r = scalars[plan.order + i]
        return pltpu.make_async_copy(ready.at[r], out.at[aligned(r * width, width), :], sems.at[r])

    def left(i, carry):
        totals = []
        for n in range(2):
            r = scalars[plan.order + jnp.minimum(begin + 2 * i + n, end - 1)]
            mirrored = apply_left(r, joined_b, lambda q, r: scalars[plan.rows + q * blocks + r], middle)
            own = dressed[aligned(r * width, width), :].astype(F32)
            totals.append((own + mirrored.astype(BF16).astype(F32)).astype(BF16))
        for n, total in enumerate(totals):
            at = begin + 2 * i + n
            ready[jnp.where(at < end, scalars[plan.order + jnp.minimum(at, end - 1)], blocks)] = total

            @pl.when(at < end)
            def _(at=at):
                leave(at).start()

        return carry

    def wait(i, carry):
        leave(i).wait()
        return carry

    lax.fori_loop(0, (end - begin + 1) // 2, left, 0)
    lax.fori_loop(begin, end, wait, 0)


def opening_kernel(plan, scalars, piece, spread_d, joined_b, dressed, middle, packed, out, token, ready, sems):
    slot, blocks = scalars[plan.mirror], joined_b.shape[0]
    rows = piece.shape[1]
    packed[...] = jnp.zeros(packed.shape, BF16)
    token[...] = jnp.zeros(token.shape, F32)
    for q in range(spread_d.shape[0]):
        apply_right(
            lambda lane: piece[slot, :, aligned(lane, LANES)],
            lambda q, s: scalars[plan.lanes + q * blocks + s],
            spread_d,
            q,
            middle,
            0,
            rows,
        )
    end = scalars[plan.begin + 1]
    finish_rows(0, end, plan, scalars, joined_b, dressed, middle, out, ready, sems)


def packed_kernel(j, last, starts, plan, scalars, spread_d, joined_b, dressed, *rest):
    pieces, rest = rest[: len(starts)], rest[len(starts) + 3 :]
    middle, packed, out, row, ready, sems = rest
    slot, factors = scalars[plan.mirror], spread_d.shape[0]
    blocks, width = joined_b.shape[:2]
    for start, piece in zip(starts, pieces):
        for lane in range(0, piece.shape[2], LANES):
            tile, at = piece[slot, :, lane : lane + LANES], start * width + lane
            packed[:, at : at + LANES] = tile
            packed[:, plan.other + at : plan.other + at + LANES] = swap_halves(tile)

    fixed = scalars[plan.whole]
    before, after = scalars[plan.whole + j - 1], scalars[plan.whole + j]
    left_half = lax.broadcasted_iota(jnp.int32, (width, LANES), 1) < width

    def take(i, carry):
        first = jnp.maximum(jnp.minimum(before + 2 * i, after - 2), fixed)
        for n in range(2):
            for k in range(0, blocks, 2):
                tiles = [packed[:, aligned(scalars[plan.slot + (first + n) * blocks + k + m], LANES)] for m in range(2)]
                row[n * width : (n + 1) * width, k * width : (k + 2) * width] = jnp.where(left_half, *tiles)
        for q in range(factors):
            uses = plan.uses + q * blocks + first
            skip = last and scalars[uses] + scalars[uses + 1] == 0

            def right(q=q):
                apply_right(
                    lambda lane: row[:, aligned(lane, LANES)],
                    lambda q, s: scalars[plan.lanes + q * blocks + s],
                    spread_d,
                    q,
                    middle,
                    pl.multiple_of(first * width, width),
                    2 * width,
                )

            if last:
                pl.when(jnp.logical_not(skip))(right)
            else:
                right()

        return carry

    lax.fori_loop(0, (after - before + 1) // 2, take, 0)
    begin, end = scalars[plan.begin + j], scalars[plan.begin + j + 1]
    finish_rows(begin, end, plan, scalars, joined_b, dressed, middle, out, ready, sems)


def mirror_piece(j, last, starts, slots, plan, scalars, pieces, spread_d, joined_b, dressed, state):
    size, (blocks, width) = dressed.shape[0], joined_b.shape[:2]
    shapes = [
        pltpu.VMEM((spread_d.shape[0], size, size), BF16),
        pltpu.VMEM((width, 2 * slots * width), BF16),
        jax.ShapeDtypeStruct((size, size), BF16),
    ]
    scratch = [pltpu.VMEM((blocks + 1, width, size), BF16), pltpu.SemaphoreType.DMA((blocks,))]
    if j == 0:
        shapes.append(jax.ShapeDtypeStruct((8, LANES), F32))
        kernel, given = functools.partial(opening_kernel, plan), (scalars, *pieces, spread_d, joined_b, dressed)
    else:
        kernel, given = functools.partial(packed_kernel, j, last, starts, plan), (scalars, spread_d, joined_b, dressed, *pieces)
        scratch = [pltpu.VMEM((2 * width, size), BF16)] + scratch
    return pl.pallas_call(
        kernel,
        in_specs=[SCALARS] + [WHOLE] * (len(given) - 1) + [WHOLE, WHOLE, FAR][: len(state)],
        out_specs=[WHOLE, WHOLE, FAR, WHOLE][: len(shapes)],
        out_shape=shapes,
        scratch_shapes=scratch,
        input_output_aliases={len(given) + i: i for i in range(len(state))},
        compiler_params=params(),
        name="mirror",
    )(*given, *state)


def cuts(blocks):
    fixed = 3 * blocks // 16
    slots = (blocks - fixed) * blocks
    return fixed, [slots * m // 208 // 2 * 2 for m in (0, 48, 96, 144, 176, 196)], slots


def later(arrays, *after):
    return lax.optimization_barrier((arrays, after))[0]


def shards(amplitudes, mirror_slot, d_values, d_cols, b_values, b_cols):
    pairs = lax.axis_size("pair")
    perm = [(i, (i + pairs // 2) % pairs) for i in range(pairs)]
    assert amplitudes.shape[0] == 1
    blocks, width = d_values.shape[1], d_values.shape[2]

    fixed, marks, slots = cuts(blocks)
    ends = [0] + marks[1:]
    layout = Layout(blocks)
    plan = Plan(lax.axis_size("fac") * d_cols.shape[0], blocks, len(ends), slots * width)
    amplitudes = pltpu.with_memory_space_constraint(amplitudes, pltpu.HBM)

    def send(piece):
        return lax.ppermute(piece, "pair", perm)

    def gather(array):
        return lax.all_gather(array, "fac", axis=0, tiled=True)

    head = turn(amplitudes, [0, fixed * width])[0]
    pieces = [[send(head)]]
    rest = turn(later(amplitudes, head), [fixed * width, blocks * width])[0]
    columns = gather(later(jnp.stack([d_cols, b_cols], axis=1), rest))
    spans = list(zip(marks, marks[1:]))
    packing, picked, over = pack_pieces(columns, [spans[0], (marks[-1], slots)], fixed, layout, rest)
    over = lax.cond(packing[layout.used + blocks] > marks[-1], send, lambda piece: piece, over)
    picked = later(picked, over)
    pieces.append([send(picked), over])
    picked = [picked, *pack_pieces(later(packing, picked), spans[1:], fixed, layout, rest)]
    d_all = gather(later(d_values, picked))
    pieces.append([send(later(picked[1], d_all))])
    b_all = gather(later(b_values, d_all))
    pieces.append([send(later(picked[2], b_all))])
    own = own_pair(fixed, ends, plan, layout, columns, packing, mirror_slot, d_all, b_all, amplitudes)
    dressed, spread_d, joined_b, scalars = own
    pieces.append([send(later(picked[3], dressed))])

    state = ()
    for j in range(len(ends)):
        if j == 1:
            *state, token = state
            pieces.append([send(later(picked[4], token))])
        arrived = pieces[j]
        starts = [] if j == 0 else [marks[j - 1], marks[-1]][: len(arrived)]
        state = mirror_piece(j, j == len(ends) - 1, starts, slots, plan, scalars, arrived, spread_d, joined_b, dressed, state)
    return state[2][None]


def solution(mesh):
    placed = (
        P(("pair", "fac"), None, None),
        P(("pair", "fac")),
        P("fac", None, None, None),
        P("fac", None),
        P("fac", None, None, None),
        P("fac", None),
    )
    return jax.shard_map(
        shards,
        mesh=mesh,
        in_specs=placed,
        out_specs=P(("pair", "fac"), None, None),
        check_vma=False,
    )
```

```python
import functools

import jax
import jax.numpy as jnp
from jax import lax
from jax.experimental import pallas as pl
from jax.experimental.pallas import tpu as pltpu
from jax.sharding import PartitionSpec as P

LANES = 128
BF16, F32 = jnp.bfloat16, jnp.float32
WHOLE = pl.BlockSpec(memory_space=pltpu.VMEM)
SCALARS = pl.BlockSpec(memory_space=pltpu.SMEM)
FAR = pl.BlockSpec(memory_space=pltpu.HBM)
VMEM_BYTES = 28 << 20


def params():
    return pltpu.CompilerParams(vmem_limit_bytes=VMEM_BYTES)


def aligned(start, size):
    return pl.ds(pl.multiple_of(start, size), size)


def strips_of(marks):
    return range(marks[0] // LANES * LANES, marks[-1], LANES)


def turn_kernel(marks, source, *rest):
    turned, strips, sems = rest[:-2], rest[-2], rest[-1]
    starts = strips_of(marks)
    copies = [
        pltpu.make_async_copy(source.at[0, :, lo : lo + LANES], strips.at[i], sems.at[i]) for i, lo in enumerate(starts)
    ]
    for copy in copies:
        copy.start()
    for i, lo in enumerate(starts):
        copies[i].wait()
        strip = strips[i].T
        for first, last, piece in zip(marks, marks[1:], turned):
            a, b = max(lo, first), min(lo + LANES, last)
            if a < b:
                piece[0, a - first : b - first, :] = strip[a - lo : b - lo, :]


def turn(amplitudes, marks):
    size = amplitudes.shape[1]
    count = len(strips_of(marks))
    return pl.pallas_call(
        functools.partial(turn_kernel, marks),
        in_specs=[FAR],
        out_specs=[WHOLE] * (len(marks) - 1),
        out_shape=[jax.ShapeDtypeStruct((1, b - a, size), BF16) for a, b in zip(marks, marks[1:])],
        scratch_shapes=[pltpu.VMEM((count, size, LANES), BF16), pltpu.SemaphoreType.DMA((count,))],
        compiler_params=params(),
        name="turn",
    )(amplitudes)


class Layout:
    def __init__(self, blocks):
        self.blocks = blocks
        self.place = 0
        self.used = blocks
        self.slot = 2 * blocks + 1
        self.block = self.slot + blocks * blocks
        self.size = self.block + blocks * blocks


def swap_halves(tile):
    half = tile.shape[1] // 2
    return jnp.concatenate([tile[:, half:], tile[:, :half]], axis=1)


def join_halves(low, low_swapped, high, high_swapped):
    low = jnp.where(low_swapped, swap_halves(low), low)
    high = jnp.where(high_swapped, swap_halves(high), high)
    lane = lax.broadcasted_iota(jnp.int32, low.shape, 1)
    return jnp.where(lane < low.shape[1] // 2, low, high)


def pack(start, piece, fixed, layout, scalars, turned):
    blocks = layout.blocks
    width = turned.shape[1] // (blocks - fixed)
    tiles = piece.shape[2] // LANES
    group = 4 if tiles % 4 == 0 else 2 if tiles % 2 == 0 else 1

    def half(slot):
        at = scalars[layout.block + slot]
        row, k = at // blocks, at % blocks
        return turned[0, aligned(row * width, width), aligned(k // 2 * LANES, LANES)], k % 2

    def fill(i, carry):
        for n in range(group):
            tile = i * group + n
            low, k_low = half(start + 2 * tile)
            high, k_high = half(start + 2 * tile + 1)
            piece[0, :, aligned(tile * LANES, LANES)] = join_halves(low, k_low == 1, high, k_high == 0)
        return carry

    lax.fori_loop(0, tiles // group, fill, 0)


def pack_kernel(starts, fixed, layout, scalars, turned, *pieces):
    for start, piece in zip(starts, pieces):
        pack(start, piece, fixed, layout, scalars, turned)


def pick_kernel(starts, fixed, layout, columns, turned, scalars, *rest):
    pieces, tally = rest[:-1], rest[-1]
    factors, blocks = columns.shape[0], columns.shape[2]

    def clear(c, carry):
        tally[c] = 0
        scalars[layout.place + c] = c
        scalars[layout.used + c] = 0
        for k in range(blocks):
            scalars[layout.block + c * blocks + k] = 0
        return carry

    def count(r, masks):
        left, right = [], []
        for q in range(factors):
            c = columns[q, 1, r]
            tally[c] = tally[c] + 1
            left.append(masks[0][q] | jnp.left_shift(1, c))
            right.append(masks[1][q] | jnp.left_shift(1, columns[q, 0, r]))
        return left, right

    lax.fori_loop(0, blocks, clear, 0)
    none = [jnp.int32(0)] * factors
    left, right = lax.fori_loop(0, blocks, count, (none, none))

    def select(at, used):
        most, c = tally[fixed], jnp.int32(fixed)
        for other in range(fixed + 1, blocks):
            n = tally[other]
            most, c = jnp.maximum(most, n), jnp.where(n > most, other, c)
        tally[c] = -2
        scalars[layout.place + c] = at
        scalars[layout.used + at] = used
        read = jnp.int32(0)
        for q in range(factors):
            read = read | jnp.where(jnp.right_shift(left[q], c) & 1 == 1, right[q], 0)
        for k in range(blocks):
            bit = jnp.right_shift(read, k) & 1
            scalars[layout.block + used] = (c - fixed) * blocks + k
            scalars[layout.slot + at * blocks + k] = jnp.where(bit == 1, used, 0)
            used = used + bit
        return used

    scalars[layout.used + blocks] = lax.fori_loop(fixed, blocks, select, jnp.int32(0))

    pack_kernel(starts, fixed, layout, scalars, turned, *pieces)


def pack_pieces(given, spans, fixed, layout, turned):
    opening = given.ndim == 3
    blocks = layout.blocks
    width = turned.shape[1] // (blocks - fixed)
    shapes = [jax.ShapeDtypeStruct((1, width, (hi - lo) * width), BF16) for lo, hi in spans]
    kernel = functools.partial(pick_kernel if opening else pack_kernel, [lo for lo, _ in spans], fixed, layout)
    return pl.pallas_call(
        kernel,
        in_specs=[SCALARS, WHOLE],
        out_specs=[SCALARS] * opening + [WHOLE] * len(spans),
        out_shape=[jax.ShapeDtypeStruct((layout.size,), jnp.int32)] * opening + shapes,
        scratch_shapes=[pltpu.SMEM((blocks,), jnp.int32)] * opening,
        compiler_params=params(),
        name="pack",
    )(given, turned)


def spread_right(values, columns, side, spread):
    factors, blocks, width = values.shape[:3]
    spread[...] = jnp.zeros(spread.shape, BF16)

    def one(group, carry):
        for q in range(factors):
            for i in range(2):
                s = 2 * group + i
                row = i * LANES + (columns[q, side, s] % 2) * width
                spread[q, group, aligned(row, width), i * width : (i + 1) * width] = values[q, s].T
        return carry

    lax.fori_loop(0, blocks // 2, one, 0)


def join_left(values, joined):
    factors, blocks, width = values.shape[:3]

    def one(r, carry):
        for q in range(factors):
            joined[r, :, q * width : (q + 1) * width] = values[q, r]
        return carry

    lax.fori_loop(0, blocks, one, 0)


def apply_right(pick, lanes, spread, q, middle, first, rows):
    for g in range(spread.shape[1]):
        picked = jnp.concatenate([pick(lanes(q, 2 * g)), pick(lanes(q, 2 * g + 1))], axis=1)
        product = jnp.dot(picked, spread[q, g], preferred_element_type=F32)
        middle[q, pl.ds(first, rows), g * LANES : (g + 1) * LANES] = product.astype(BF16)


def apply_left(r, joined, starts, middle):
    factors, width = middle.shape[0], joined.shape[1]
    picked = [middle[q, aligned(starts(q, r), width), :] for q in range(factors)]
    return jnp.dot(joined[r], jnp.concatenate(picked, axis=0), preferred_element_type=F32)


class Plan:
    def __init__(self, factors, blocks, pieces, other):
        self.blocks = blocks
        self.other = other
        self.lanes = 0
        self.rows = factors * blocks
        self.uses = 2 * factors * blocks
        self.slot = 3 * factors * blocks
        self.whole = self.slot + blocks * blocks
        self.order = self.whole + pieces
        self.begin = self.order + blocks
        self.mirror = self.begin + pieces + 1
        self.size = self.mirror + 1


def make_plan(fixed, ends, plan, layout, columns, packing, slot, scalars):
    factors, blocks = columns.shape[0], columns.shape[2]

    def clear(i, carry):
        scalars[plan.uses + i] = 0
        return carry

    def offsets(s, carry):
        for q in range(factors):
            at = packing[layout.place + columns[q, 1, s]]
            scalars[plan.lanes + q * blocks + s] = columns[q, 0, s] // 2 * LANES
            scalars[plan.rows + q * blocks + s] = at * (LANES // 2)
            use = plan.uses + q * blocks + at
            scalars[use] = scalars[use] + 1
        return carry

    def locate(i, carry):
        for n in range(2):
            at = packing[layout.slot + 2 * i + n]
            scalars[plan.slot + 2 * i + n] = (at + n) % 2 * plan.other + at // 2 * LANES
        return carry

    lax.fori_loop(0, factors * blocks, clear, 0)
    lax.fori_loop(0, blocks, offsets, 0)
    lax.fori_loop(fixed * blocks // 2, blocks * blocks // 2, locate, 0)
    found, low = jnp.int32(0), jnp.int32(0)
    for j, end in enumerate(ends):

        def ready(at, n, end=end):
            return n + (jnp.minimum(packing[layout.used + at + 1], ends[-1]) <= end).astype(jnp.int32)

        high = lax.fori_loop(fixed, blocks, ready, jnp.int32(fixed)) if j else jnp.int32(fixed)
        scalars[plan.whole + j] = high
        scalars[plan.begin + j] = found

        def one(r, found, low=low, high=high):
            last = packing[layout.place + columns[0, 1, r]]
            for q in range(1, factors):
                last = jnp.maximum(last, packing[layout.place + columns[q, 1, r]])
            here = jnp.logical_and(last >= low, last < high)

            @pl.when(here)
            def _():
                scalars[plan.order + found] = r

            return found + here.astype(jnp.int32)

        found, low = lax.fori_loop(0, blocks, one, found), high
    scalars[plan.begin + len(ends)] = found
    scalars[plan.mirror] = slot[0]


def own_kernel(
    fixed,
    ends,
    plan,
    layout,
    columns,
    packing,
    slot,
    d_all,
    b_all,
    source,
    dressed,
    spread_d,
    joined_b,
    scalars,
    spread_b,
    joined_d,
    middle,
):
    factors, blocks, width = d_all.shape[:3]
    size = source.shape[1]
    make_plan(fixed, ends, plan, layout, columns, packing, slot, scalars)
    spread_right(b_all, columns, 1, spread_b)
    join_left(d_all, joined_d)
    spread_right(d_all, columns, 0, spread_d)
    join_left(b_all, joined_b)
    step = min(256, size)

    def right(q, carry):
        for m in range(0, size, step):
            apply_right(
                lambda lane: source[0, m : m + step, aligned(lane, LANES)],
                lambda q, s: columns[q, 1, s] // 2 * LANES,
                spread_b,
                q,
                middle,
                m,
                step,
            )
        return carry

    def left(r, carry):
        block = apply_left(r, joined_d, lambda q, r: columns[q, 0, r] * width, middle)
        dressed[aligned(r * width, width), :] = block.astype(BF16)
        return carry

    lax.fori_loop(0, factors, right, 0)
    lax.fori_loop(0, blocks, left, 0)


def own_pair(fixed, ends, plan, layout, columns, packing, slot, d_all, b_all, amplitudes):
    factors, blocks, width = d_all.shape[:3]
    size = amplitudes.shape[1]
    spread = (factors, blocks // 2, 2 * LANES, LANES)
    joined = (blocks, width, factors * width)
    return pl.pallas_call(
        functools.partial(own_kernel, fixed, ends, plan, layout),
        in_specs=[SCALARS, SCALARS, SCALARS, WHOLE, WHOLE, WHOLE],
        out_specs=[WHOLE, WHOLE, WHOLE, SCALARS],
        out_shape=[
            pltpu.VMEM((size, size), BF16),
            pltpu.VMEM(spread, BF16),
            pltpu.VMEM(joined, BF16),
            pltpu.SMEM((plan.size,), jnp.int32),
        ],
        scratch_shapes=[
            pltpu.VMEM(spread, BF16),
            pltpu.VMEM(joined, BF16),
            pltpu.VMEM((factors, size, size), BF16),
        ],
        compiler_params=params(),
        name="own",
    )(columns, packing, slot, d_all, b_all, amplitudes)


def finish_rows(begin, end, plan, scalars, joined_b, dressed, middle, out, ready, sems):
    blocks, width = joined_b.shape[:2]

    def leave(i):
        r = scalars[plan.order + i]
        return pltpu.make_async_copy(ready.at[r], out.at[aligned(r * width, width), :], sems.at[r])

    def left(i, carry):
        totals = []
        for n in range(2):
            r = scalars[plan.order + jnp.minimum(begin + 2 * i + n, end - 1)]
            mirrored = apply_left(r, joined_b, lambda q, r: scalars[plan.rows + q * blocks + r], middle)
            own = dressed[aligned(r * width, width), :].astype(F32)
            totals.append((own + mirrored.astype(BF16).astype(F32)).astype(BF16))
        for n, total in enumerate(totals):
            at = begin + 2 * i + n
            ready[jnp.where(at < end, scalars[plan.order + jnp.minimum(at, end - 1)], blocks)] = total

            @pl.when(at < end)
            def _(at=at):
                leave(at).start()

        return carry

    def wait(i, carry):
        leave(i).wait()
        return carry

    lax.fori_loop(0, (end - begin + 1) // 2, left, 0)
    lax.fori_loop(begin, end, wait, 0)


def opening_kernel(plan, scalars, piece, spread_d, joined_b, dressed, middle, packed, out, token, ready, sems):
    slot, blocks = scalars[plan.mirror], joined_b.shape[0]
    rows = piece.shape[1]
    packed[...] = jnp.zeros(packed.shape, BF16)
    token[...] = jnp.zeros(token.shape, F32)
    for q in range(spread_d.shape[0]):
        apply_right(
            lambda lane: piece[slot, :, aligned(lane, LANES)],
            lambda q, s: scalars[plan.lanes + q * blocks + s],
            spread_d,
            q,
            middle,
            0,
            rows,
        )
    end = scalars[plan.begin + 1]
    finish_rows(0, end, plan, scalars, joined_b, dressed, middle, out, ready, sems)


def packed_kernel(j, last, starts, plan, scalars, spread_d, joined_b, dressed, *rest):
    pieces, rest = rest[: len(starts)], rest[len(starts) + 3 :]
    middle, packed, out, row, ready, sems = rest
    slot, factors = scalars[plan.mirror], spread_d.shape[0]
    blocks, width = joined_b.shape[:2]
    for start, piece in zip(starts, pieces):
        for lane in range(0, piece.shape[2], LANES):
            tile, at = piece[slot, :, lane : lane + LANES], start * width + lane
            packed[:, at : at + LANES] = tile
            packed[:, plan.other + at : plan.other + at + LANES] = swap_halves(tile)

    fixed = scalars[plan.whole]
    before, after = scalars[plan.whole + j - 1], scalars[plan.whole + j]
    left_half = lax.broadcasted_iota(jnp.int32, (width, LANES), 1) < width

    def take(i, carry):
        first = jnp.maximum(jnp.minimum(before + 2 * i, after - 2), fixed)
        for n in range(2):
            for k in range(0, blocks, 2):
                tiles = [packed[:, aligned(scalars[plan.slot + (first + n) * blocks + k + m], LANES)] for m in range(2)]
                row[n * width : (n + 1) * width, k * width : (k + 2) * width] = jnp.where(left_half, *tiles)
        for q in range(factors):
            uses = plan.uses + q * blocks + first
            skip = last and jnp.where(first >= before, scalars[uses], 0) + scalars[uses + 1] == 0

            def right(q=q):
                apply_right(
                    lambda lane: row[:, aligned(lane, LANES)],
                    lambda q, s: scalars[plan.lanes + q * blocks + s],
                    spread_d,
                    q,
                    middle,
                    pl.multiple_of(first * width, width),
                    2 * width,
                )

            if last:
                pl.when(jnp.logical_not(skip))(right)
            else:
                right()

        return carry

    lax.fori_loop(0, (after - before + 1) // 2, take, 0)
    begin, end = scalars[plan.begin + j], scalars[plan.begin + j + 1]
    finish_rows(begin, end, plan, scalars, joined_b, dressed, middle, out, ready, sems)


def mirror_piece(j, last, starts, slots, plan, scalars, pieces, spread_d, joined_b, dressed, state):
    size, (blocks, width) = dressed.shape[0], joined_b.shape[:2]
    shapes = [
        pltpu.VMEM((spread_d.shape[0], size, size), BF16),
        pltpu.VMEM((width, 2 * slots * width), BF16),
        jax.ShapeDtypeStruct((size, size), BF16),
    ]
    scratch = [pltpu.VMEM((blocks + 1, width, size), BF16), pltpu.SemaphoreType.DMA((blocks,))]
    if j == 0:
        shapes.append(jax.ShapeDtypeStruct((8, LANES), F32))
        kernel, given = functools.partial(opening_kernel, plan), (scalars, *pieces, spread_d, joined_b, dressed)
    else:
        kernel, given = functools.partial(packed_kernel, j, last, starts, plan), (scalars, spread_d, joined_b, dressed, *pieces)
        scratch = [pltpu.VMEM((2 * width, size), BF16)] + scratch
    return pl.pallas_call(
        kernel,
        in_specs=[SCALARS] + [WHOLE] * (len(given) - 1) + [WHOLE, WHOLE, FAR][: len(state)],
        out_specs=[WHOLE, WHOLE, FAR, WHOLE][: len(shapes)],
        out_shape=shapes,
        scratch_shapes=scratch,
        input_output_aliases={len(given) + i: i for i in range(len(state))},
        compiler_params=params(),
        name="mirror",
    )(*given, *state)


def cuts(blocks):
    fixed = 3 * blocks // 16
    slots = (blocks - fixed) * blocks
    return fixed, [slots * m // 208 // 2 * 2 for m in (0, 48, 96, 144, 176, 196)], slots


def later(arrays, *after):
    return lax.optimization_barrier((arrays, after))[0]


def shards(amplitudes, mirror_slot, d_values, d_cols, b_values, b_cols):
    pairs = lax.axis_size("pair")
    perm = [(i, (i + pairs // 2) % pairs) for i in range(pairs)]
    assert amplitudes.shape[0] == 1
    blocks, width = d_values.shape[1], d_values.shape[2]

    fixed, marks, slots = cuts(blocks)
    ends = [0] + marks[1:]
    layout = Layout(blocks)
    plan = Plan(lax.axis_size("fac") * d_cols.shape[0], blocks, len(ends), slots * width)
    amplitudes = pltpu.with_memory_space_constraint(amplitudes, pltpu.HBM)

    def send(piece):
        return lax.ppermute(piece, "pair", perm)

    def gather(array):
        return lax.all_gather(array, "fac", axis=0, tiled=True)

    head = turn(amplitudes, [0, fixed * width])[0]
    pieces = [[send(head)]]
    rest = turn(later(amplitudes, head), [fixed * width, blocks * width])[0]
    columns = gather(later(jnp.stack([d_cols, b_cols], axis=1), rest))
    spans = list(zip(marks, marks[1:]))
    packing, picked, over = pack_pieces(columns, [spans[0], (marks[-1], slots)], fixed, layout, rest)
    over = lax.cond(packing[layout.used + blocks] > marks[-1], send, lambda piece: piece, over)
    picked = later(picked, over)
    pieces.append([send(picked), over])
    picked = [picked, *pack_pieces(later(packing, picked), spans[1:], fixed, layout, rest)]
    d_all = gather(later(d_values, picked))
    pieces.append([send(later(picked[1], d_all))])
    b_all = gather(later(b_values, d_all))
    pieces.append([send(later(picked[2], b_all))])
    own = own_pair(fixed, ends, plan, layout, columns, packing, mirror_slot, d_all, b_all, amplitudes)
    dressed, spread_d, joined_b, scalars = own
    pieces.append([send(later(picked[3], dressed))])

    state = ()
    for j in range(len(ends)):
        if j == 1:
            *state, token = state
            pieces.append([send(later(picked[4], token))])
        arrived = pieces[j]
        starts = [] if j == 0 else [marks[j - 1], marks[-1]][: len(arrived)]
        state = mirror_piece(j, j == len(ends) - 1, starts, slots, plan, scalars, arrived, spread_d, joined_b, dressed, state)
    return state[2][None]


def solution(mesh):
    placed = (
        P(("pair", "fac"), None, None),
        P(("pair", "fac")),
        P("fac", None, None, None),
        P("fac", None),
        P("fac", None, None, None),
        P("fac", None),
    )
    return jax.shard_map(
        shards,
        mesh=mesh,
        in_specs=placed,
        out_specs=P(("pair", "fac"), None, None),
        check_vma=False,
    )
```
